256 devices in a mesh: dp: 32 (over x, z), section: 2 (over core), mp: 4 (over y).
Axes of the slice: x: 4, y: 4, z: 8, core: 2. Of those that a mesh axis runs over, the one named last changes fastest.
Arguments:
- tokens: bfloat16 [8192, 4096], P('dp', 'mp'), may hold values from -18 to 18
- passages: bfloat16 [160, 128, 4096], P('dp', None, 'mp'), may hold values from -18 to 18
- weights: bfloat16 [2, 2, 4096, 2048], P('section', None, None, 'mp'), may hold values from -0.09375 to 0.09375
- cotangent: bfloat16 [8192, 4096], P('dp', 'mp'), may hold values from -6 to 6
- neighbours: int32 [128, 2], P('dp'), may hold values from 0 to 6, as said below
- passage_home: int32 [160], replicated, may hold values from 0 to 159, as said below
- request_lists: int32 [32, 7], replicated, may hold values from 0 to 159, as said below
Outputs:
- token_grad: bfloat16 [8192, 4096], P('dp', ('section', 'mp'))
- passage_grad: bfloat16 [160, 128, 4096], P('dp', None, ('section', 'mp'))
The draws below stay inside these ranges and needn't reach their ends.
Inputs may be any that keep to these rules, and one draw needn't show every extreme that they name: `request_lists`: row j holds 7 distinct passage ids; at most 1 of them are stored on one index of dp (storage row passage_home[id] // 5), and in every row exactly 1 are stored on some index. `passage_home`: A permutation of the passage ids. Every position of row c // 4 of request_lists is named by some block of that dp index; the two neighbours of a block may coincide.
All inputs are finite; a program needn't handle non-finite values.
Results may differ from the reference program's by a relative error of at most 0.015.
The reference program's roundings to bfloat16 on the way count: a program that leaves them out, or rounds other values in their place, can miss the bound.
Values may be sent and summed in bfloat16 or wider, within the bound.
No kernel may reach another device: no remote copies, remote signals or barrier semaphores. Data moves between devices by JAX's collectives and lax.ppermute only.
A program may use at most 128 MiB of HBM per device.

```python
import math
import jax
import jax.numpy as jnp
from jax import lax

D = 4096
HEADS = 16
HEAD_DIM = 128
BLOCK = 64
NBR = 2
NBR_LEN = 128
BLOCKS_DEV = 4
P_DEV = 5
HD = 2048
U_DEV = 7
SLOTS = 1
BLOCKS = 128
TOKENS = 8192
PASSAGES = 160
N_DP = 32
N_MP = 4


def distinct_order(key, array_shape):
    scores = jax.random.randint(key, array_shape, 0, 1 << 20) * array_shape[-1]
    scores = scores + jnp.arange(array_shape[-1], dtype=jnp.int32)
    return jnp.argsort(scores, axis=-1, stable=True).astype(jnp.int32)


def routing(key):
    keys_all = jax.random.split(key, 6)
    home_rows = jax.random.permutation(keys_all[0], PASSAGES).astype(jnp.int32)
    stored_ids = jnp.zeros((PASSAGES,), jnp.int32).at[home_rows].set(jnp.arange(PASSAGES, dtype=jnp.int32))
    owner_order = distinct_order(keys_all[1], (N_DP, N_DP))
    local_order = distinct_order(keys_all[2], (N_DP, N_DP, P_DEV))
    remainder = U_DEV - SLOTS
    other_count = max(N_DP - 1, 1)
    positions = jnp.arange(N_DP, dtype=jnp.int32)
    counts = jnp.where(positions == 0, SLOTS, remainder // other_count + (positions - 1 < remainder % other_count).astype(jnp.int32))
    end_points = jnp.cumsum(counts).astype(jnp.int32)
    start_points = end_points - counts
    entries = jnp.arange(U_DEV, dtype=jnp.int32)
    rank_of = jnp.sum((end_points[None, :] <= entries[:, None]).astype(jnp.int32), axis=1)
    within = entries - start_points[rank_of]
    owners = owner_order[:, rank_of]
    requesters = jnp.arange(N_DP, dtype=jnp.int32)[:, None]
    local_rows = local_order[requesters, owners, within[None, :]]
    id_lists = stored_ids[owners * P_DEV + local_rows]
    id_lists = jnp.take_along_axis(id_lists, distinct_order(keys_all[3], (N_DP, U_DEV)), axis=1)
    ref_count = NBR * BLOCKS_DEV
    ref_base = jnp.concatenate([jnp.broadcast_to(entries, (N_DP, U_DEV)), jax.random.randint(keys_all[4], (N_DP, ref_count - U_DEV), 0, U_DEV)], axis=1)
    ref_lists = jnp.take_along_axis(ref_base, distinct_order(keys_all[5], (N_DP, ref_count)), axis=1)
    return (home_rows, id_lists.astype(jnp.int32), ref_lists.reshape(BLOCKS, NBR).astype(jnp.int32))


def scaled_rows(key, array_shape, loud_scale):
    normal_key, choice_key = jax.random.split(key)
    normal_part = jnp.clip(jax.random.normal(normal_key, array_shape, jnp.float32), -6.0, 6.0)
    chosen = jax.random.randint(choice_key, array_shape[:-1] + (1,), 0, 8) == 0
    return (normal_part * jnp.where(chosen, loud_scale, 1.0)).astype(jnp.bfloat16)


def draw_passage_home(key, part):
    home_rows, id_lists, ref_lists = routing(key)
    return home_rows


def draw_request_lists(key, part):
    home_rows, id_lists, ref_lists = routing(key)
    return id_lists


def draw_neighbours(key, part):
    home_rows, id_lists, ref_lists = routing(key)
    return ref_lists


def draw_tokens(key, part):
    key = jax.random.fold_in(key, 5)
    loud_scale = 1.0
    return scaled_rows(key, (TOKENS, D), loud_scale)


def draw_passages(key, part):
    key = jax.random.fold_in(key, 7)
    loud_scale = 1.0
    return scaled_rows(key, (PASSAGES, NBR_LEN, D), loud_scale)


def steps_of(rng, dims, cuts, smallest, largest):
    def one(position, shards_of):
        draws = jax.random.uniform(jax.random.fold_in(jax.random.fold_in(rng, 6), position), (shards_of,), jnp.float32, smallest / len(cuts), largest / len(cuts))
        return jnp.repeat(jnp.exp(draws), dims[position] // shards_of).reshape((-1,) + (1,) * (len(dims) - position - 1))

    loudness = one(*cuts[0])
    for cut in cuts[1:]:
        loudness = loudness * one(*cut)
    return loudness


def gaussian(rng, extent, deviation, limit, shards=(), held_as=jnp.bfloat16):
    values = jax.random.normal(rng, extent, jnp.float32) * deviation
    if len(shards) > 0:
        values = steps_of(rng, extent, shards, -0.22, 0.18) * values
    return jnp.clip(values, min=-limit, max=limit).astype(held_as)


def setup_inputs(seed: int = 0) -> dict:
    streams_of = jax.random.split(jax.random.key(seed), 8)
    return {
        "tokens": draw_tokens(jax.random.fold_in(streams_of[7], 71), 0),
        "passages": draw_passages(jax.random.fold_in(streams_of[7], 71), 0),
        "weights": gaussian(streams_of[2], (2, 2, D, HD), D ** -0.5, 0.09375, ((0, 2), (3, 4))),
        "cotangent": gaussian(streams_of[3], (TOKENS, D), 1.0, 6.0, ((0, 32), (1, 4))),
        "neighbours": draw_neighbours(jax.random.fold_in(streams_of[7], 71), 0),
        "passage_home": draw_passage_home(jax.random.fold_in(streams_of[7], 71), 0),
        "request_lists": draw_request_lists(jax.random.fold_in(streams_of[7], 71), 0),
    }


def contract(left, right):
    return lax.dot_general(left, right, (((1,), (1,)), ((), ())), preferred_element_type=jnp.float32)

def reference(tokens, passages, weights, cotangent, neighbours, passage_home, request_lists):
    w_key = weights[0, 0]
    w_value = weights[0, 1]
    w_query = weights[1, 0]
    w_out = weights[1, 1]
    flattened = passages.reshape(PASSAGES * NBR_LEN, D)
    all_keys = jnp.dot(flattened, w_key, preferred_element_type=jnp.float32).astype(jnp.bfloat16).reshape(PASSAGES, NBR_LEN, HD)
    all_values = jnp.dot(flattened, w_value, preferred_element_type=jnp.float32).astype(jnp.bfloat16).reshape(PASSAGES, NBR_LEN, HD)
    queries = jnp.dot(tokens, w_query, preferred_element_type=jnp.float32).astype(jnp.bfloat16)
    ctx_grad = jnp.dot(cotangent, w_out, preferred_element_type=jnp.float32).astype(jnp.bfloat16)
    store_rows = jnp.take(passage_home, request_lists, axis=0)
    block_rows = BLOCKS_DEV * BLOCK
    score_scale = 1.0 / math.sqrt(HEAD_DIM)
    highest = lax.Precision.HIGHEST

    def per_device(device_index):
        query_part = lax.dynamic_slice_in_dim(queries, device_index * block_rows, block_rows, 0)
        query_part = query_part.astype(jnp.float32).reshape(BLOCKS_DEV, BLOCK, HEADS, HEAD_DIM)
        grad_part = lax.dynamic_slice_in_dim(ctx_grad, device_index * block_rows, block_rows, 0)
        grad_part = grad_part.astype(jnp.float32).reshape(BLOCKS_DEV, BLOCK, HEADS, HEAD_DIM)
        pointers = lax.dynamic_slice_in_dim(neighbours, device_index * BLOCKS_DEV, BLOCKS_DEV, 0).reshape(-1)
        my_rows = jnp.take(store_rows, device_index, axis=0)
        attended = jnp.take(my_rows, pointers, axis=0)
        key_part = jnp.take(all_keys, attended, axis=0).astype(jnp.float32).reshape(BLOCKS_DEV, NBR * NBR_LEN, HEADS, HEAD_DIM)
        value_part = jnp.take(all_values, attended, axis=0).astype(jnp.float32).reshape(BLOCKS_DEV, NBR * NBR_LEN, HEADS, HEAD_DIM)
        scores = jnp.einsum('cqhd,ckhd->chqk', query_part, key_part, precision=highest) * score_scale
        probs = jax.nn.softmax(scores, axis=-1)
        probs_round = lax.optimization_barrier(probs.astype(jnp.bfloat16)).astype(jnp.float32)
        prob_grad = jnp.einsum('cqhd,ckhd->chqk', grad_part, value_part, precision=highest)
        inner_sum = lax.optimization_barrier(jnp.sum(probs * prob_grad, axis=-1, keepdims=True))
        score_grad = (probs * (prob_grad - inner_sum) * score_scale).astype(jnp.bfloat16)
        score_grad = lax.optimization_barrier(score_grad).astype(jnp.float32)
        query_grad = jnp.einsum('chqk,ckhd->cqhd', score_grad, key_part, precision=highest)
        query_grad = query_grad.astype(jnp.bfloat16).reshape(block_rows, HD)
        key_term = jnp.einsum('chqk,cqhd->ckhd', score_grad, query_part, precision=highest).reshape(BLOCKS_DEV * NBR, NBR_LEN * HD)
        value_term = jnp.einsum('chqk,cqhd->ckhd', probs_round, grad_part, precision=highest).reshape(BLOCKS_DEV * NBR, NBR_LEN * HD)
        member = (jnp.arange(U_DEV, dtype=jnp.int32)[:, None] == pointers[None, :]).astype(jnp.float32)
        list_keys = jnp.dot(member, key_term, precision=highest).astype(jnp.bfloat16).reshape(U_DEV, NBR_LEN, HD)
        list_values = jnp.dot(member, value_term, precision=highest).astype(jnp.bfloat16).reshape(U_DEV, NBR_LEN, HD)
        return (query_grad, list_keys, list_values)
    query_grads, list_keys, list_values = lax.map(per_device, jnp.arange(N_DP, dtype=jnp.int32))
    store_ids = store_rows.reshape(-1)
    key_total = jax.ops.segment_sum(list_keys.reshape(N_DP * U_DEV, NBR_LEN, HD).astype(jnp.float32), store_ids, num_segments=PASSAGES)
    value_total = jax.ops.segment_sum(list_values.reshape(N_DP * U_DEV, NBR_LEN, HD).astype(jnp.float32), store_ids, num_segments=PASSAGES)
    key_flat = key_total.astype(jnp.bfloat16).reshape(PASSAGES * NBR_LEN, HD)
    value_flat = value_total.astype(jnp.bfloat16).reshape(PASSAGES * NBR_LEN, HD)
    flat_grads = query_grads.reshape(TOKENS, HD)
    group_cols = HD // N_MP
    token_sum = jnp.zeros((TOKENS, D), jnp.float32)
    passage_sum = jnp.zeros((PASSAGES * NBR_LEN, D), jnp.float32)
    for group_index in range(N_MP):
        lower = group_index * group_cols
        upper = lower + group_cols
        token_part = contract(flat_grads[:, lower:upper], w_query[:, lower:upper])
        token_sum = token_sum + lax.optimization_barrier(token_part.astype(jnp.bfloat16)).astype(jnp.float32)
        passage_part = contract(key_flat[:, lower:upper], w_key[:, lower:upper]) + contract(value_flat[:, lower:upper], w_value[:, lower:upper])
        passage_sum = passage_sum + lax.optimization_barrier(passage_part.astype(jnp.bfloat16)).astype(jnp.float32)
    return (token_sum.astype(jnp.bfloat16), passage_sum.reshape(PASSAGES, NBR_LEN, D).astype(jnp.bfloat16))
```

```python
import math

import jax
import jax.numpy as jnp
from jax import lax
from jax.experimental import pallas as pl
from jax.experimental.pallas import tpu as pltpu
from jax.sharding import PartitionSpec as P

HEAD_DIM = 128
BLOCK = 64
SCALE = 1.0 / math.sqrt(HEAD_DIM)
UNUSED = 1e30
VMEM = pl.BlockSpec(memory_space=pltpu.VMEM)
SMEM = pl.BlockSpec(memory_space=pltpu.SMEM)
PARAMS = pltpu.CompilerParams(vmem_limit_bytes=40 * 1024 * 1024)


def rows_by_rows(left, right):
    return lax.dot_general(left, right, (((1,), (1,)), ((), ())), preferred_element_type=jnp.float32)


def spread_kernel(block_of, rows_ref, out_ref, sems):
    count = out_ref.shape[0]
    copies = [
        pltpu.make_async_copy(rows_ref.at[block_of[slot]], out_ref.at[slot], sems.at[slot])
        for slot in range(count)
    ]
    for copy in copies:
        copy.start()
    for copy in copies:
        copy.wait()


def spread(block_of, blocks):
    count = block_of.shape[0]
    return pl.pallas_call(
        spread_kernel,
        out_shape=jax.ShapeDtypeStruct((count,) + blocks.shape[1:], blocks.dtype),
        in_specs=[SMEM, VMEM],
        out_specs=pl.BlockSpec(memory_space=pl.ANY),
        scratch_shapes=[pltpu.SemaphoreType.DMA((count,))],
        compiler_params=PARAMS,
    )(block_of, blocks)


def head_views(rows_ref, kv_ref, j, passage, head, heads):
    width = heads * HEAD_DIM
    first = pl.ds(head * HEAD_DIM, HEAD_DIM)
    second = pl.ds(width + head * HEAD_DIM, HEAD_DIM)
    return (
        rows_ref[j, :, first],
        rows_ref[j, :, second],
        kv_ref[passage, :, first],
        kv_ref[passage, :, second],
    )


def stats_kernel(count, lists, local, rows_ref, kv_ref, out_ref):
    heads = rows_ref.shape[2] // (2 * HEAD_DIM)
    out_ref[...] = jnp.zeros_like(out_ref)

    def one_list(i, carry):
        j, passage = (lists[i], local[i])
        for head in range(heads):
            query, grad, key, value = head_views(rows_ref, kv_ref, j, passage, head, heads)
            scores = rows_by_rows(key, query) * SCALE
            prob_grad = rows_by_rows(value, grad)
            top = jnp.max(scores, axis=0, keepdims=True)
            raised = jnp.exp(scores - top)
            total = jnp.sum(raised, axis=0, keepdims=True)
            inner = jnp.sum(raised * prob_grad, axis=0, keepdims=True) / total
            out_ref[j, 2 * head : 2 * head + 1, :] = top + jnp.log(total)
            out_ref[j, 2 * head + 1 : 2 * head + 2, :] = inner
        return carry

    lax.fori_loop(0, count[0], one_list, 0)


def list_stats(routes, rows, kv):
    return pl.pallas_call(
        stats_kernel,
        out_shape=jax.ShapeDtypeStruct((rows.shape[0], 8, rows.shape[1]), jnp.float32),
        in_specs=[SMEM, SMEM, SMEM, VMEM, VMEM],
        out_specs=VMEM,
        compiler_params=PARAMS,
    )(*routes, rows, kv)


def combine_kernel(owner_of, slot_of, stats_ref, out_ref):
    sub = lax.broadcasted_iota(jnp.int32, stats_ref.shape[1:], 0)
    lane = lax.broadcasted_iota(jnp.int32, stats_ref.shape[1:], 1)
    even = sub % 2 == 0
    out_ref[...] = jnp.broadcast_to(jnp.where(even, UNUSED, 0.0)[None], out_ref.shape)
    for block in range(owner_of.shape[0] // 2):
        refs = (2 * block, 2 * block + 1)
        logs, inners = ([], [])
        for ref in refs:
            row = stats_ref[owner_of[ref]]
            row = jnp.where(slot_of[ref] == 0, row, pltpu.roll(row, BLOCK, 1))
            logs.append(row)
            inners.append(pltpu.roll(row, 7, 0))
        top = jnp.maximum(logs[0], logs[1])
        first, second = (jnp.exp(logs[0] - top), jnp.exp(logs[1] - top))
        total = first + second
        joint = (first * inners[0] + second * inners[1]) / total
        both = jnp.where(even, top + jnp.log(total), pltpu.roll(joint, 1, 0))
        both = jnp.where(lane < BLOCK, both, pltpu.roll(both, BLOCK, 1))
        for ref in refs:
            place = owner_of[ref]
            half = jnp.where(lane < BLOCK, 0, 1)
            out_ref[place] = jnp.where(half == slot_of[ref], both, out_ref[place])


def combine(owner_of, slot_of, stats):
    return pl.pallas_call(
        combine_kernel,
        out_shape=jax.ShapeDtypeStruct(stats.shape, jnp.float32),
        in_specs=[SMEM, SMEM, VMEM],
        out_specs=VMEM,
        compiler_params=PARAMS,
    )(owner_of, slot_of, stats)


def grads_kernel(
    count, lists, local, rows_ref, kv_ref, joint_ref, query_out, stored_out, total
):
    heads = rows_ref.shape[2] // (2 * HEAD_DIM)
    width = heads * HEAD_DIM
    total[...] = jnp.zeros_like(total)
    query_out[...] = jnp.zeros_like(query_out)

    def add_rounded(passage, low, term):
        place = (passage, slice(None), pl.ds(low, HEAD_DIM))
        total[place] += term.astype(jnp.bfloat16).astype(jnp.float32)

    def one_list(i, carry):
        j, passage = (lists[i], local[i])
        for head in range(heads):
            low = head * HEAD_DIM
            query, grad, key, value = head_views(rows_ref, kv_ref, j, passage, head, heads)
            scores = rows_by_rows(key, query) * SCALE
            prob_grad = rows_by_rows(value, grad)
            probs = jnp.exp(scores - joint_ref[j, 2 * head : 2 * head + 1, :])
            inner = joint_ref[j, 2 * head + 1 : 2 * head + 2, :]
            score_grad = (probs * (prob_grad - inner) * SCALE).astype(jnp.bfloat16)
            query_grad = lax.dot_general(
                score_grad, key, (((0,), (0,)), ((), ())), preferred_element_type=jnp.float32
            )
            query_out[j, :, pl.ds(low, HEAD_DIM)] = query_grad.astype(jnp.bfloat16)
            add_rounded(
                passage, low, jnp.dot(score_grad, query, preferred_element_type=jnp.float32)
            )
            add_rounded(
                passage,
                width + low,
                jnp.dot(probs.astype(jnp.bfloat16), grad, preferred_element_type=jnp.float32),
            )
        return carry

    lax.fori_loop(0, count[0], one_list, 0)
    stored_out[...] = total[...].astype(jnp.bfloat16)


def list_grads(routes, rows, kv, joint):
    return pl.pallas_call(
        grads_kernel,
        out_shape=(
            jax.ShapeDtypeStruct((rows.shape[0], rows.shape[1], rows.shape[2] // 2), jnp.bfloat16),
            jax.ShapeDtypeStruct(kv.shape, jnp.bfloat16),
        ),
        in_specs=[SMEM, SMEM, SMEM, VMEM, VMEM, VMEM],
        out_specs=(VMEM, VMEM),
        scratch_shapes=[pltpu.VMEM(kv.shape, jnp.float32)],
        compiler_params=PARAMS,
    )(*routes, rows, kv, joint)


def swapped(value):
    return lax.ppermute(value, "section", [(0, 1), (1, 0)])


def turned(value, steps):
    count = lax.axis_size("mp")
    return lax.ppermute(value, "mp", [(i, (i + steps) % count) for i in range(count)])


def exchanged(value):
    return lax.all_to_all(value, "dp", split_axis=0, concat_axis=0, tiled=True)


def per_device(tokens, passages, weights, cotangent, neighbours, passage_home, request_lists):
    own_index = lax.axis_index("dp")
    section = lax.axis_index("section")
    group = lax.axis_index("mp")
    groups = lax.axis_size("mp")
    peers = lax.axis_size("dp")
    leading = section == 0
    per_owner, length, width = passages.shape
    head_cols = weights.shape[3]
    half = head_cols // 2
    row_count = tokens.shape[0]
    block_count = neighbours.shape[0]

    own = weights[0]
    other = swapped(own)

    def by_section(first, second):
        return lax.cond(leading, first, second, own, other)

    store_rows = jnp.take(passage_home, request_lists, axis=0)
    mine = store_rows // per_owner == own_index
    wanted = jnp.any(mine, axis=1)
    held_at = jnp.max(jnp.where(mine, store_rows % per_owner, 0), axis=1)
    turn = jnp.sum(wanted[None, :] & (jnp.arange(peers)[None, :] < jnp.arange(peers)[:, None]), axis=1)
    chosen = wanted[None, :] & (turn[None, :] == jnp.arange(peers)[:, None])
    routes = (
        jnp.sum(wanted.astype(jnp.int32)).reshape(1),
        jnp.max(jnp.where(chosen, jnp.arange(peers)[None, :], 0), axis=1).astype(jnp.int32),
        jnp.max(jnp.where(chosen, held_at[None, :], 0), axis=1).astype(jnp.int32),
    )
    pointers = neighbours.reshape(-1)
    my_rows = lax.dynamic_index_in_dim(store_rows, own_index, 0, False)
    owner_of = jnp.take(my_rows, pointers, axis=0) // per_owner
    refs = jnp.arange(pointers.shape[0])
    earlier = (pointers[None, :] == pointers[:, None]) & (refs[None, :] < refs[:, None])
    slot_of = jnp.minimum(jnp.sum(earlier.astype(jnp.int32), axis=1), 1)
    places = owner_of * 2 + slot_of
    block_of = jnp.max(
        jnp.where(places[None, :] == jnp.arange(2 * peers)[:, None], refs[None, :] // 2, 0), axis=1
    ).astype(jnp.int32)

    start = jnp.where(leading, tokens, cotangent)
    token_parts = [start] + [turned(start, k) for k in range(1, groups)]

    def project(parts, matrices):
        results = []
        for matrix in matrices:
            total = None
            for k, part in enumerate(parts):
                low = (group - k) % groups * width
                rows = lax.dynamic_slice_in_dim(matrix, low, width, 0)
                term = jnp.dot(part, rows, preferred_element_type=jnp.float32)
                total = term if total is None else total + term
            results.append(total.astype(jnp.bfloat16))
        return results

    projected = by_section(
        lambda a, b: project(token_parts, [b[0]])[0], lambda a, b: project(token_parts, [a[1]])[0]
    )
    kept = jnp.where(leading, projected[:, :half], projected[:, half:])
    got = swapped(jnp.where(leading, projected[:, half:], projected[:, :half]))
    rows = jnp.concatenate(
        [jnp.where(leading, kept, got), jnp.where(leading, got, kept)], axis=1
    ).reshape(block_count, BLOCK, 2 * half)
    slots = spread(block_of, rows)
    asked = exchanged(slots.reshape(peers, 2 * BLOCK, 2 * half))

    flat = passages.reshape(per_owner * length, width)
    half_rows = per_owner * length // 2
    held = lax.dynamic_slice_in_dim(flat, section * half_rows, half_rows, 0)
    held, _ = lax.optimization_barrier((held, token_parts))
    held_parts = [held] + [turned(held, k) for k in range(1, groups)]
    keys, values = by_section(
        lambda a, b: project(held_parts, [a[0], a[1]]), lambda a, b: project(held_parts, [b[0], b[1]])
    )

    def heads_of(which):
        return jnp.concatenate(
            [
                lax.dynamic_slice_in_dim(keys, which * half, half, 1),
                lax.dynamic_slice_in_dim(values, which * half, half, 1),
            ],
            axis=1,
        )

    kv_mine = heads_of(section)
    kv_got = swapped(heads_of(1 - section))
    kv = jnp.concatenate(
        [jnp.where(leading, kv_mine, kv_got), jnp.where(leading, kv_got, kv_mine)], axis=0
    ).reshape(per_owner, length, 2 * half)

    joint = exchanged(combine(owner_of, slot_of, exchanged(list_stats(routes, asked, kv))))
    query_slots, stored = list_grads(routes, asked, kv, joint)
    returned = exchanged(query_slots).reshape(2 * peers, BLOCK, half)

    def summed(terms):
        total = terms[0].astype(jnp.float32)
        for k in range(1, groups):
            total = total + turned(terms[k], k).astype(jnp.float32)
        return total.astype(jnp.bfloat16)

    def to_features(pairs):
        terms = []
        for k in range(groups):
            chunk = width // 2
            low = section * (groups * chunk) + (group + k) % groups * chunk
            term = None
            for grads, matrix in pairs:
                part = rows_by_rows(grads, lax.dynamic_slice_in_dim(matrix, low, chunk, 0))
                term = part if term is None else term + part
            terms.append(term.astype(jnp.bfloat16))
        return terms

    stored = stored.reshape(per_owner * length, 2 * half)
    stored_got = swapped(stored)
    lower = jnp.where(leading, stored, stored_got)
    upper = jnp.where(leading, stored_got, stored)
    key_grad = jnp.concatenate([lower[:, :half], upper[:, :half]], axis=1)
    value_grad = jnp.concatenate([lower[:, half:], upper[:, half:]], axis=1)
    passage_terms = by_section(
        lambda a, b: to_features([(key_grad, a[0]), (value_grad, a[1])]),
        lambda a, b: to_features([(key_grad, b[0]), (value_grad, b[1])]),
    )
    passage_grad = summed(passage_terms).reshape(per_owner, length, width // 2)

    terms = jnp.take(returned, places, axis=0).reshape(block_count, 2, BLOCK, half)
    query_grad = (terms[:, 0].astype(jnp.float32) + terms[:, 1].astype(jnp.float32)).astype(
        jnp.bfloat16
    )
    query_grad = query_grad.reshape(row_count, half)
    query_got = swapped(query_grad)
    query_grad = jnp.concatenate(
        [jnp.where(leading, query_grad, query_got), jnp.where(leading, query_got, query_grad)],
        axis=1,
    )
    token_terms = by_section(
        lambda a, b: to_features([(query_grad, b[0])]), lambda a, b: to_features([(query_grad, a[0])])
    )
    return (summed(token_terms), passage_grad)


def solution(mesh):
    in_specs = (
        P("dp", "mp"),
        P("dp", None, "mp"),
        P("section", None, None, "mp"),
        P("dp", "mp"),
        P("dp", None),
        P(),
        P(),
    )
    out_specs = (P("dp", ("section", "mp")), P("dp", None, ("section", "mp")))
    return jax.shard_map(
        per_device, mesh=mesh, in_specs=in_specs, out_specs=out_specs, check_vma=False
    )
```

```python
import math

import jax
import jax.numpy as jnp
from jax import lax
from jax.experimental import pallas as pl
from jax.experimental.pallas import tpu as pltpu
from jax.sharding import PartitionSpec as P

HEAD_DIM = 128
BLOCK = 64
X_CHIPS = 4
Z_CHIPS = 8
SCALE = 1.0 / math.sqrt(HEAD_DIM)
UNUSED = 1e30
VMEM = pl.BlockSpec(memory_space=pltpu.VMEM)
SMEM = pl.BlockSpec(memory_space=pltpu.SMEM)
ANY = pl.BlockSpec(memory_space=pl.ANY)
PARAMS = pltpu.CompilerParams(vmem_limit_bytes=56 * 1024 * 1024)


def cost(flops, moved):
    return pl.CostEstimate(flops=int(flops), bytes_accessed=int(moved), transcendentals=0)


def rows_by_rows(left, right):
    return lax.dot_general(left, right, (((1,), (1,)), ((), ())), preferred_element_type=jnp.float32)


def start_by_section(section, choices, copy_from):
    for which, weights_ref in enumerate(choices):

        @pl.when(section == which)
        def _():
            copy_from(which, weights_ref).start()


def project_kernel(picks, here, own_ref, other_ref, *refs):
    parts = refs[:4]
    keep_ref, send_ref, held, sems = refs[4:]
    section, group = (here[0], here[1])
    depth = parts[0].shape[1]
    mats = len(picks[0][1])
    half = held.shape[3] // 2

    def fetch(which, source, mat, k):
        low = pl.multiple_of((group - k + 4) % 4 * depth, depth)
        return pltpu.make_async_copy(
            source.at[picks[which][1][mat], pl.ds(low, depth), :],
            held.at[mat, k],
            sems.at[mat * 4 + k],
        )

    for k in range(4):
        for mat in range(mats):
            start_by_section(
                section,
                [own_ref if picks[which][0] else other_ref for which in range(2)],
                lambda which, source: fetch(which, source, mat, k),
            )
    for mat in range(mats):
        total = None
        for k in range(4):
            fetch(0, own_ref, mat, k).wait()
            term = jnp.dot(parts[k][...], held[mat, k], preferred_element_type=jnp.float32)
            total = term if total is None else total + term
        low, high = (total[:, :half].astype(jnp.bfloat16), total[:, half:].astype(jnp.bfloat16))
        columns = pl.ds(mat * half, half)

        @pl.when(section == 0)
        def _():
            keep_ref[:, columns] = low
            send_ref[:, columns] = high

        @pl.when(section == 1)
        def _():
            keep_ref[:, columns] = high
            send_ref[:, columns] = low


def project(picks, here, own, other, parts):
    rows, depth = parts[0].shape
    mats = len(picks[0][1])
    cols = own.shape[2]
    out = jax.ShapeDtypeStruct((rows, mats * cols // 2), jnp.bfloat16)
    return pl.pallas_call(
        lambda *refs: project_kernel(picks, *refs),
        out_shape=(out, out),
        in_specs=[SMEM, ANY, ANY] + [VMEM] * 4,
        out_specs=(VMEM, VMEM),
        scratch_shapes=[
            pltpu.VMEM((mats, 4, depth, cols), jnp.bfloat16),
            pltpu.SemaphoreType.DMA((mats * 4,)),
        ],
        compiler_params=PARAMS,
        cost_estimate=cost(8 * rows * depth * cols * mats, 8 * depth * cols * mats),
    )(here, own, other, *parts)


def features_kernel(picks, here, own_ref, other_ref, mine_ref, got_ref, *refs):
    outs = refs[:4]
    held, sems = refs[4:]
    section, group = (here[0], here[1])
    mats, _, _, chunk, half = held.shape

    def fetch(which, source, mat, side, k):
        low = pl.multiple_of((section * 4 + (group + k) % 4) * chunk, chunk)
        left = which * half if side == 0 else (1 - which) * half
        return pltpu.make_async_copy(
            source.at[picks[which][1][mat], pl.ds(low, chunk), pl.ds(left, half)],
            held.at[mat, side, k],
            sems.at[(mat * 2 + side) * 4 + k],
        )

    order = (2, 1, 3, 0)
    for k in order:
        for mat in range(mats):
            for side in range(2):
                start_by_section(
                    section,
                    [own_ref if picks[which][0] else other_ref for which in range(2)],
                    lambda which, source: fetch(which, source, mat, side, k),
                )
    for k in order:
        total = None
        for mat in range(mats):
            for side, grads in enumerate((mine_ref, got_ref)):
                fetch(0, own_ref, mat, side, k).wait()
                term = rows_by_rows(grads[:, mat * half : (mat + 1) * half], held[mat, side, k])
                total = term if total is None else total + term
        outs[k][...] = total.astype(jnp.bfloat16)


def features(picks, here, own, other, mine, got):
    rows = mine.shape[0]
    mats = len(picks[0][1])
    half = mine.shape[1] // mats
    chunk = own.shape[1] // 8
    out = jax.ShapeDtypeStruct((rows, chunk), jnp.bfloat16)
    return pl.pallas_call(
        lambda *refs: features_kernel(picks, *refs),
        out_shape=(out,) * 4,
        in_specs=[SMEM, ANY, ANY, VMEM, VMEM],
        out_specs=(VMEM,) * 4,
        scratch_shapes=[
            pltpu.VMEM((mats, 2, 4, chunk, half), jnp.bfloat16),
            pltpu.SemaphoreType.DMA((mats * 8,)),
        ],
        compiler_params=PARAMS,
        cost_estimate=cost(16 * rows * chunk * half * mats, 16 * chunk * half * mats),
    )(here, own, other, mine, got)


def head_views(rows_ref, kv_ref, i, passage, head, heads):
    width = heads * HEAD_DIM
    first = pl.ds(head * HEAD_DIM, HEAD_DIM)
    second = pl.ds(width + head * HEAD_DIM, HEAD_DIM)
    return (
        rows_ref[i, :, first],
        rows_ref[i, :, second],
        kv_ref[passage, :, first],
        kv_ref[passage, :, second],
    )


def stats_kernel(count, lists, local, blocks, unit, place, near_ref, *refs):
    far_refs = refs[: Z_CHIPS + 1]
    kv_ref, rows_ref, out_ref, sems = refs[Z_CHIPS + 1 :]
    heads = rows_ref.shape[2] // (2 * HEAD_DIM)
    held = near_ref.shape[1] // BLOCK
    out_ref[...] = jnp.zeros_like(out_ref)

    def fetch(source, first, row, i, slot):
        low = pl.multiple_of(row * BLOCK, BLOCK)
        return pltpu.make_async_copy(
            source.at[first, pl.ds(low, BLOCK), :],
            rows_ref.at[i, pl.ds(slot * BLOCK, BLOCK), :],
            sems.at[2 * i + slot],
        )

    def ask(i, carry):
        for slot in range(2):
            block = blocks[2 * i + slot]

            @pl.when(block < held)
            def _():
                fetch(near_ref, lists[i], block, i, slot).start()

            for which, far_ref in enumerate(far_refs):

                @pl.when((block >= held) & (unit[i] == which))
                def _():
                    fetch(far_ref, place[i], block - held, i, slot).start()

        return carry

    lax.fori_loop(0, count[0], ask, 0)

    def one_list(i, carry):
        j, passage = (lists[i], local[i])
        for slot in range(2):
            fetch(near_ref, 0, 0, i, slot).wait()
        for head in range(heads):
            query, grad, key, value = head_views(rows_ref, kv_ref, i, passage, head, heads)
            scores = rows_by_rows(key, query) * SCALE
            prob_grad = rows_by_rows(value, grad)
            top = jnp.max(scores, axis=0, keepdims=True)
            raised = jnp.exp(scores - top)
            total = jnp.sum(raised, axis=0, keepdims=True)
            inner = jnp.sum(raised * prob_grad, axis=0, keepdims=True) / total
            out_ref[j, 2 * head : 2 * head + 1, :] = top + jnp.log(total)
            out_ref[j, 2 * head + 1 : 2 * head + 2, :] = inner
        return carry

    lax.fori_loop(0, count[0], one_list, 0)


def list_stats(routes, sources, near, far, kv):
    lists = routes[1].shape[0]
    return pl.pallas_call(
        stats_kernel,
        out_shape=(
            jax.ShapeDtypeStruct((lists, 2 * BLOCK, near.shape[2]), jnp.bfloat16),
            jax.ShapeDtypeStruct((lists, 8, 2 * BLOCK), jnp.float32),
        ),
        in_specs=[SMEM] * 6 + [ANY] * (Z_CHIPS + 2) + [VMEM],
        out_specs=(VMEM, VMEM),
        scratch_shapes=[pltpu.SemaphoreType.DMA((2 * lists,))],
        compiler_params=PARAMS,
    )(*routes, *sources, near, *far, kv)


def combine_kernel(owner_of, slot_of, stats_ref, out_ref):
    sub = lax.broadcasted_iota(jnp.int32, stats_ref.shape[1:], 0)
    lane = lax.broadcasted_iota(jnp.int32, stats_ref.shape[1:], 1)
    even = sub % 2 == 0
    out_ref[...] = jnp.broadcast_to(jnp.where(even, UNUSED, 0.0)[None], out_ref.shape)
    for block in range(owner_of.shape[0] // 2):
        refs = (2 * block, 2 * block + 1)
        logs, inners = ([], [])
        for ref in refs:
            row = stats_ref[owner_of[ref]]
            row = jnp.where(slot_of[ref] == 0, row, pltpu.roll(row, BLOCK, 1))
            logs.append(row)
            inners.append(pltpu.roll(row, 7, 0))
        top = jnp.maximum(logs[0], logs[1])
        first, second = (jnp.exp(logs[0] - top), jnp.exp(logs[1] - top))
        total = first + second
        joint = (first * inners[0] + second * inners[1]) / total
        both = jnp.where(even, top + jnp.log(total), pltpu.roll(joint, 1, 0))
        both = jnp.where(lane < BLOCK, both, pltpu.roll(both, BLOCK, 1))
        for ref in refs:
            place = owner_of[ref]
            half = jnp.where(lane < BLOCK, 0, 1)
            out_ref[place] = jnp.where(half == slot_of[ref], both, out_ref[place])


def combine(owner_of, slot_of, stats):
    return pl.pallas_call(
        combine_kernel,
        out_shape=jax.ShapeDtypeStruct(stats.shape, jnp.float32),
        in_specs=[SMEM, SMEM, VMEM],
        out_specs=VMEM,
        compiler_params=PARAMS,
    )(owner_of, slot_of, stats)


def score_terms(rows_ref, kv_ref, joint_ref, i, j, passage, head, heads):
    query, grad, key, value = head_views(rows_ref, kv_ref, i, passage, head, heads)
    scores = rows_by_rows(key, query) * SCALE
    prob_grad = rows_by_rows(value, grad)
    probs = jnp.exp(scores - joint_ref[j, 2 * head : 2 * head + 1, :])
    inner = joint_ref[j, 2 * head + 1 : 2 * head + 2, :]
    score_grad = (probs * (prob_grad - inner) * SCALE).astype(jnp.bfloat16)
    return (query, grad, key, probs, score_grad)


def query_kernel(count, lists, local, rows_ref, kv_ref, joint_ref, query_out):
    heads = rows_ref.shape[2] // (2 * HEAD_DIM)
    query_out[...] = jnp.zeros_like(query_out)

    def one_list(i, carry):
        j, passage = (lists[i], local[i])
        for head in range(heads):
            _, _, key, _, score_grad = score_terms(
                rows_ref, kv_ref, joint_ref, i, j, passage, head, heads
            )
            query_grad = lax.dot_general(
                score_grad, key, (((0,), (0,)), ((), ())), preferred_element_type=jnp.float32
            )
            query_out[j, :, pl.ds(head * HEAD_DIM, HEAD_DIM)] = query_grad.astype(jnp.bfloat16)
        return carry

    lax.fori_loop(0, count[0], one_list, 0)


def list_queries(routes, rows, kv, joint):
    return pl.pallas_call(
        query_kernel,
        out_shape=jax.ShapeDtypeStruct(
            (rows.shape[0], rows.shape[1], rows.shape[2] // 2), jnp.bfloat16
        ),
        in_specs=[SMEM] * 3 + [VMEM] * 3,
        out_specs=VMEM,
        compiler_params=PARAMS,
    )(*routes, rows, kv, joint)


def stored_kernel(count, lists, local, rows_ref, kv_ref, joint_ref, stored_out, total):
    heads = rows_ref.shape[2] // (2 * HEAD_DIM)
    width = heads * HEAD_DIM
    total[...] = jnp.zeros_like(total)

    def add_rounded(passage, low, term):
        place = (passage, slice(None), pl.ds(low, HEAD_DIM))
        total[place] += term.astype(jnp.bfloat16).astype(jnp.float32)

    def one_list(i, carry):
        j, passage = (lists[i], local[i])
        for head in range(heads):
            low = head * HEAD_DIM
            query, grad, _, probs, score_grad = score_terms(
                rows_ref, kv_ref, joint_ref, i, j, passage, head, heads
            )
            add_rounded(
                passage, low, jnp.dot(score_grad, query, preferred_element_type=jnp.float32)
            )
            add_rounded(
                passage,
                width + low,
                jnp.dot(probs.astype(jnp.bfloat16), grad, preferred_element_type=jnp.float32),
            )
        return carry

    lax.fori_loop(0, count[0], one_list, 0)
    stored_out[...] = total[...].astype(jnp.bfloat16)


def list_stored(routes, rows, kv, joint):
    return pl.pallas_call(
        stored_kernel,
        out_shape=jax.ShapeDtypeStruct(kv.shape, jnp.bfloat16),
        in_specs=[SMEM] * 3 + [VMEM] * 3,
        out_specs=VMEM,
        scratch_shapes=[pltpu.VMEM(kv.shape, jnp.float32)],
        compiler_params=PARAMS,
        cost_estimate=cost(8 * rows.size * HEAD_DIM, 4 * rows.size),
    )(*routes, rows, kv, joint)


def swapped(value):
    return lax.ppermute(value, "section", [(0, 1), (1, 0)])


def turned(value, steps):
    count = lax.axis_size("mp")
    return lax.ppermute(value, "mp", [(i, (i + steps) % count) for i in range(count)])


def exchanged(value):
    return lax.all_to_all(value, "dp", split_axis=0, concat_axis=0, tiled=True)


def along_x(value, steps):
    pairs = [
        (x * Z_CHIPS + z, (x + steps) % X_CHIPS * Z_CHIPS + z)
        for x in range(X_CHIPS)
        for z in range(Z_CHIPS)
    ]
    return lax.ppermute(value, "dp", pairs)


def along_z(value, steps):
    pairs = [
        (x * Z_CHIPS + z, x * Z_CHIPS + (z + steps) % Z_CHIPS)
        for x in range(X_CHIPS)
        for z in range(Z_CHIPS)
    ]
    return lax.ppermute(value, "dp", pairs)


def gathered_near(value):
    columns = [[x * Z_CHIPS + z for z in range(Z_CHIPS)] for x in range(X_CHIPS)]
    rows = [[x * Z_CHIPS + z for x in range(X_CHIPS)] for z in range(Z_CHIPS)]
    column = lax.all_gather(value, "dp", axis=0, tiled=True, axis_index_groups=columns)
    return lax.all_gather(column, "dp", axis=0, tiled=True, axis_index_groups=rows)


def gathered_far(value):
    unit = jnp.stack([value] + [along_x(value, k) for k in range(1, X_CHIPS)])
    units = [None] * (Z_CHIPS + 1)
    units[0] = unit
    ahead = behind = unit
    for step in range(1, Z_CHIPS // 2):
        ahead, behind = (along_z(ahead, 1), along_z(behind, -1))
        units[Z_CHIPS - step], units[step] = (ahead, behind)
    middle = X_CHIPS // 2
    units[Z_CHIPS // 2] = along_z(ahead[:middle], 1)
    units[Z_CHIPS] = along_z(behind[middle:], -1)
    return units


KEY_VALUE = ((True, (0, 1)), (False, (0, 1)))
QUERY_OUT = ((False, (0,)), (True, (1,)))
QUERY = ((False, (0,)), (True, (0,)))


def per_device(tokens, passages, weights, cotangent, neighbours, passage_home, request_lists):
    own_index = lax.axis_index("dp")
    section = lax.axis_index("section")
    group = lax.axis_index("mp")
    groups = lax.axis_size("mp")
    peers = lax.axis_size("dp")
    leading = section == 0
    per_owner, length, width = passages.shape
    half = weights.shape[3] // 2
    row_count = tokens.shape[0]
    block_count = neighbours.shape[0]
    here = jnp.stack([section, group]).astype(jnp.int32)

    start = jnp.where(leading, tokens, cotangent)
    token_parts = [start] + [turned(start, k) for k in range(1, groups)]
    own = weights[0]
    other = swapped(own)

    pointers = neighbours.reshape(-1)
    refs = jnp.arange(pointers.shape[0])
    shown = jnp.pad(pointers, (0, 2 * BLOCK - pointers.shape[0]))
    shown = exchanged(jnp.broadcast_to(shown[None, None, :], (peers, 8, 2 * BLOCK)))
    all_pointers = shown[:, 0, : pointers.shape[0]]
    store_rows = jnp.take(passage_home, request_lists, axis=0)
    mine = store_rows // per_owner == own_index
    wanted = jnp.any(mine, axis=1)
    held_at = jnp.max(jnp.where(mine, store_rows % per_owner, 0), axis=1)
    position = jnp.max(jnp.where(mine, jnp.arange(store_rows.shape[1])[None, :], 0), axis=1)
    naming = all_pointers == position[:, None]
    last_ref = pointers.shape[0] - 1
    first_block = jnp.min(jnp.where(naming, refs[None, :], last_ref), axis=1) // 2
    second_block = jnp.max(jnp.where(naming, refs[None, :], 0), axis=1) // 2
    peer = jnp.arange(peers)
    turn = jnp.sum(wanted[None, :] & (peer[None, :] < peer[:, None]), axis=1)
    chosen = wanted[None, :] & (turn[None, :] == peer[:, None])

    def compacted(values):
        return jnp.max(jnp.where(chosen, values[None, :], 0), axis=1).astype(jnp.int32)

    lists = compacted(peer)
    routes = (jnp.sum(wanted.astype(jnp.int32)).reshape(1), lists, compacted(held_at))
    behind_z = (lists % Z_CHIPS - own_index % Z_CHIPS) % Z_CHIPS
    behind_x = (own_index // Z_CHIPS - lists // Z_CHIPS) % X_CHIPS
    split = (behind_z == Z_CHIPS // 2) & (behind_x >= X_CHIPS // 2)
    sources = (
        jnp.stack([compacted(first_block), compacted(second_block)], axis=1).reshape(-1),
        jnp.where(split, Z_CHIPS, behind_z).astype(jnp.int32),
        jnp.where(split, behind_x - X_CHIPS // 2, behind_x).astype(jnp.int32),
    )
    my_rows = lax.dynamic_index_in_dim(store_rows, own_index, 0, False)
    owner_of = jnp.take(my_rows, pointers, axis=0) // per_owner
    earlier = (pointers[None, :] == pointers[:, None]) & (refs[None, :] < refs[:, None])
    slot_of = jnp.minimum(jnp.sum(earlier.astype(jnp.int32), axis=1), 1)
    places = owner_of * 2 + slot_of

    kept, sent = project(QUERY_OUT, here, own, other, token_parts)
    got = swapped(sent)
    rows = jnp.concatenate(
        [jnp.where(leading, kept, got), jnp.where(leading, got, kept)], axis=1
    )
    near = gathered_near(rows[: row_count // 2]).reshape(peers, row_count // 2, 2 * half)
    far = gathered_far(rows[row_count // 2 :])

    flat = passages.reshape(per_owner * length, width)
    half_rows = per_owner * length // 2
    held = lax.dynamic_slice_in_dim(flat, section * half_rows, half_rows, 0)
    held, _ = lax.optimization_barrier((held, token_parts))
    held_parts = [held] + [turned(held, k) for k in range(1, groups)]
    kept, sent = project(KEY_VALUE, here, own, other, held_parts)
    got = swapped(sent)
    kv = jnp.concatenate(
        [jnp.where(leading, kept, got), jnp.where(leading, got, kept)], axis=0
    ).reshape(per_owner, length, 2 * half)

    asked, stats = list_stats(routes, sources, near, far, kv)
    joint = exchanged(combine(owner_of, slot_of, exchanged(stats)))
    query_slots = list_queries(routes, asked, kv, joint)
    returned = exchanged(query_slots).reshape(2 * peers, BLOCK, half)
    stored = list_stored(routes, asked, kv, joint)

    def summed(terms):
        total = terms[0].astype(jnp.float32)
        for k in range(1, groups):
            total = total + turned(terms[k], k).astype(jnp.float32)
        return total.astype(jnp.bfloat16)

    stored = stored.reshape(per_owner * length, 2 * half)
    passage_terms = features(KEY_VALUE, here, own, other, stored, swapped(stored))
    passage_grad = summed(passage_terms).reshape(per_owner, length, width // 2)

    terms = jnp.take(returned, places, axis=0).reshape(block_count, 2, BLOCK, half)
    query_grad = (terms[:, 0].astype(jnp.float32) + terms[:, 1].astype(jnp.float32)).astype(
        jnp.bfloat16
    )
    query_grad = query_grad.reshape(row_count, half)
    token_terms = features(QUERY, here, own, other, query_grad, swapped(query_grad))
    return (summed(token_terms), passage_grad)


def solution(mesh):
    in_specs = (
        P("dp", "mp"),
        P("dp", None, "mp"),
        P("section", None, None, "mp"),
        P("dp", "mp"),
        P("dp", None),
        P(),
        P(),
    )
    out_specs = (P("dp", ("section", "mp")), P("dp", None, ("section", "mp")))
    return jax.shard_map(
        per_device, mesh=mesh, in_specs=in_specs, out_specs=out_specs, check_vma=False
    )
```

```python
import math

import jax
import jax.numpy as jnp
from jax import lax
from jax.experimental import pallas as pl
from jax.experimental.pallas import tpu as pltpu
from jax.sharding import PartitionSpec as P

HEAD_DIM = 128
BLOCK = 64
X_CHIPS = 4
Z_CHIPS = 8
SCALE = 1.0 / math.sqrt(HEAD_DIM)
UNUSED = 1e30
VMEM = pl.BlockSpec(memory_space=pltpu.VMEM)
SMEM = pl.BlockSpec(memory_space=pltpu.SMEM)
ANY = pl.BlockSpec(memory_space=pl.ANY)
PARAMS = pltpu.CompilerParams(vmem_limit_bytes=56 * 1024 * 1024)


def cost(flops, moved):
    return pl.CostEstimate(flops=int(flops), bytes_accessed=int(moved), transcendentals=0)


def rows_by_rows(left, right):
    return lax.dot_general(left, right, (((1,), (1,)), ((), ())), preferred_element_type=jnp.float32)


def routing_kernel(
    per_owner, here, home, wanted, shown, count, lists, local, blocks, line, unit, place, owner_of, slot_of
):
    peers, listed = wanted.shape
    refs = shown.shape[1]
    own = here[2]
    lowest = own * per_owner
    own_x, own_z = (lax.div(own, Z_CHIPS), lax.rem(own, Z_CHIPS))

    def one_list(j, found):
        position, held_at = (-1, 0)
        for u in range(listed):
            row = home[wanted[j, u]] - lowest
            hit = (row >= 0) & (row < per_owner)
            position = jnp.where(hit, u, position)
            held_at = jnp.where(hit, row, held_at)

        behind_z = lax.rem(lax.rem(j, Z_CHIPS) - own_z + Z_CHIPS, Z_CHIPS)
        behind_x = lax.rem(own_x - lax.div(j, Z_CHIPS) + X_CHIPS, X_CHIPS)
        row = lax.div(j, Z_CHIPS) * Z_CHIPS + behind_z

        @pl.when(position >= 0)
        def _():
            first, last = (refs - 1, 0)
            for ref in range(refs):
                last = jnp.where(shown[row, ref] == position, ref, last)
                back = refs - 1 - ref
                first = jnp.where(shown[row, back] == position, back, first)
            lists[found] = j
            local[found] = held_at
            blocks[2 * found] = lax.div(first, 2)
            blocks[2 * found + 1] = lax.div(last, 2)
            line[found] = row
            split = (behind_z == Z_CHIPS // 2) & (behind_x >= X_CHIPS // 2)
            unit[found] = jnp.where(split, Z_CHIPS, behind_z)
            place[found] = jnp.where(split, behind_x - X_CHIPS // 2, behind_x)

        return found + jnp.where(position >= 0, 1, 0)

    count[0] = lax.fori_loop(0, peers, one_list, 0)
    for ref in range(refs):
        pointer = shown[own_x * Z_CHIPS, ref]
        owner_of[ref] = lax.div(home[wanted[own, pointer]], per_owner)
        slot = 0
        for before in range(ref):
            slot = jnp.where(shown[own_x * Z_CHIPS, before] == pointer, 1, slot)
        slot_of[ref] = slot


def routing(here, home, wanted, shown, per_owner):
    peers, refs = shown.shape
    sizes = (1, peers, peers, 2 * peers, peers, peers, peers, refs, refs)
    return pl.pallas_call(
        lambda *args: routing_kernel(per_owner, *args),
        out_shape=tuple(jax.ShapeDtypeStruct((size,), jnp.int32) for size in sizes),
        in_specs=[SMEM] * 4,
        out_specs=(SMEM,) * len(sizes),
        compiler_params=PARAMS,
    )(here, home, wanted, shown)


def start_by_section(section, choices, copy_from):
    for which, weights_ref in enumerate(choices):

        @pl.when(section == which)
        def _():
            copy_from(which, weights_ref).start()


def project_kernel(picks, here, own_ref, other_ref, *refs):
    parts = refs[:4]
    keep_ref, send_ref, held, sems = refs[-4:]
    section, group = (here[0], here[1])
    depth = parts[0].shape[1]
    mats = len(picks[0][1])
    half = held.shape[3] // 2

    def fetch(which, source, mat, k):
        low = pl.multiple_of((group - k + 4) % 4 * depth, depth)
        return pltpu.make_async_copy(
            source.at[picks[which][1][mat], pl.ds(low, depth), :],
            held.at[mat, k],
            sems.at[mat * 4 + k],
        )

    for k in range(4):
        for mat in range(mats):
            start_by_section(
                section,
                [own_ref if picks[which][0] else other_ref for which in range(2)],
                lambda which, source: fetch(which, source, mat, k),
            )
    for mat in range(mats):
        total = None
        for k in range(4):
            fetch(0, own_ref, mat, k).wait()
            term = jnp.dot(parts[k][...], held[mat, k], preferred_element_type=jnp.float32)
            total = term if total is None else total + term
        low, high = (total[:, :half].astype(jnp.bfloat16), total[:, half:].astype(jnp.bfloat16))
        columns = pl.ds(mat * half, half)

        @pl.when(section == 0)
        def _():
            keep_ref[:, columns] = low
            send_ref[:, columns] = high

        @pl.when(section == 1)
        def _():
            keep_ref[:, columns] = high
            send_ref[:, columns] = low


def project(picks, here, own, other, parts, after=()):
    rows, depth = parts[0].shape
    mats = len(picks[0][1])
    cols = own.shape[2]
    out = jax.ShapeDtypeStruct((rows, mats * cols // 2), jnp.bfloat16)
    return pl.pallas_call(
        lambda *refs: project_kernel(picks, *refs),
        out_shape=(out, out),
        in_specs=[SMEM, ANY, ANY] + [VMEM] * 4 + [ANY] * len(after),
        out_specs=(VMEM, VMEM),
        scratch_shapes=[
            pltpu.VMEM((mats, 4, depth, cols), jnp.bfloat16),
            pltpu.SemaphoreType.DMA((mats * 4,)),
        ],
        compiler_params=PARAMS,
        cost_estimate=cost(8 * rows * depth * cols * mats, 8 * depth * cols * mats),
    )(here, own, other, *parts, *after)


def features_kernel(picks, here, own_ref, other_ref, mine_ref, got_ref, *refs):
    outs = refs[:4]
    held, sems = refs[4:]
    section, group = (here[0], here[1])
    mats, _, _, chunk, half = held.shape

    def fetch(which, source, mat, side, k):
        low = pl.multiple_of((section * 4 + (group + k) % 4) * chunk, chunk)
        left = which * half if side == 0 else (1 - which) * half
        return pltpu.make_async_copy(
            source.at[picks[which][1][mat], pl.ds(low, chunk), pl.ds(left, half)],
            held.at[mat, side, k],
            sems.at[(mat * 2 + side) * 4 + k],
        )

    order = (2, 1, 3, 0)
    for k in order:
        for mat in range(mats):
            for side in range(2):
                start_by_section(
                    section,
                    [own_ref if picks[which][0] else other_ref for which in range(2)],
                    lambda which, source: fetch(which, source, mat, side, k),
                )
    for k in order:
        total = None
        for mat in range(mats):
            for side, grads in enumerate((mine_ref, got_ref)):
                fetch(0, own_ref, mat, side, k).wait()
                term = rows_by_rows(grads[:, mat * half : (mat + 1) * half], held[mat, side, k])
                total = term if total is None else total + term
        outs[k][...] = total.astype(jnp.bfloat16)


def features(picks, here, own, other, mine, got):
    rows = mine.shape[0]
    mats = len(picks[0][1])
    half = mine.shape[1] // mats
    chunk = own.shape[1] // 8
    out = jax.ShapeDtypeStruct((rows, chunk), jnp.bfloat16)
    return pl.pallas_call(
        lambda *refs: features_kernel(picks, *refs),
        out_shape=(out,) * 4,
        in_specs=[SMEM, ANY, ANY, VMEM, VMEM],
        out_specs=(VMEM,) * 4,
        scratch_shapes=[
            pltpu.VMEM((mats, 2, 4, chunk, half), jnp.bfloat16),
            pltpu.SemaphoreType.DMA((mats * 8,)),
        ],
        compiler_params=PARAMS,
        cost_estimate=cost(16 * rows * chunk * half * mats, 16 * chunk * half * mats),
    )(here, own, other, mine, got)


def head_views(rows_ref, kv_ref, i, passage, head, heads):
    width = heads * HEAD_DIM
    first = pl.ds(head * HEAD_DIM, HEAD_DIM)
    second = pl.ds(width + head * HEAD_DIM, HEAD_DIM)
    return (
        rows_ref[i, :, first],
        rows_ref[i, :, second],
        kv_ref[passage, :, first],
        kv_ref[passage, :, second],
    )


def chains(first, second, heads):
    return [(item, head) for item in (first, second) for head in range(heads)]


def over_pairs(count, body):
    def step(t, carry):
        return body(2 * t, jnp.minimum(2 * t + 1, count - 1), carry)

    lax.fori_loop(0, lax.div(count + 1, 2), step, 0)


def stats_kernel(count, lists, local, blocks, line, unit, place, near_ref, *refs):
    far_refs = refs[: Z_CHIPS + 1]
    kv_ref, rows_ref, out_ref, sems = refs[Z_CHIPS + 1 :]
    heads = rows_ref.shape[2] // (2 * HEAD_DIM)
    held = near_ref.shape[1] // BLOCK
    out_ref[...] = jnp.zeros_like(out_ref)

    def fetch(source, first, row, i, slot):
        low = pl.multiple_of(row * BLOCK, BLOCK)
        return pltpu.make_async_copy(
            source.at[first, pl.ds(low, BLOCK), :],
            rows_ref.at[i, pl.ds(slot * BLOCK, BLOCK), :],
            sems.at[2 * i + slot],
        )

    def ask(i, carry):
        for slot in range(2):
            block = blocks[2 * i + slot]

            @pl.when(block < held)
            def _():
                fetch(near_ref, line[i], block, i, slot).start()

            for which, far_ref in enumerate(far_refs):

                @pl.when((block >= held) & (unit[i] == which))
                def _():
                    fetch(far_ref, place[i], block - held, i, slot).start()

        return carry

    lax.fori_loop(0, count[0], ask, 0)

    def one_pair(i, second, carry):
        for slot in range(2):
            fetch(near_ref, 0, 0, i, slot).wait()

        @pl.when(second > i)
        def _():
            for slot in range(2):
                fetch(near_ref, 0, 0, second, slot).wait()

        found = []
        for item, head in chains(i, second, heads):
            query, grad, key, value = head_views(rows_ref, kv_ref, item, local[item], head, heads)
            scores = rows_by_rows(key, query) * SCALE
            prob_grad = rows_by_rows(value, grad)
            top = jnp.max(scores, axis=0, keepdims=True)
            raised = jnp.exp(scores - top)
            total = jnp.sum(raised, axis=0, keepdims=True)
            inner = jnp.sum(raised * prob_grad, axis=0, keepdims=True) / total
            found.append((item, head, top + jnp.log(total), inner))
        for item, head, logs, inner in found:
            out_ref[lists[item], 2 * head : 2 * head + 1, :] = logs
            out_ref[lists[item], 2 * head + 1 : 2 * head + 2, :] = inner
        return carry

    over_pairs(count[0], one_pair)


def list_stats(routes, sources, near, far, kv):
    lists = routes[1].shape[0]
    return pl.pallas_call(
        stats_kernel,
        out_shape=(
            jax.ShapeDtypeStruct((lists, 2 * BLOCK, near.shape[2]), jnp.bfloat16),
            jax.ShapeDtypeStruct((lists, 8, 2 * BLOCK), jnp.float32),
        ),
        in_specs=[SMEM] * 7 + [ANY] * (Z_CHIPS + 2) + [VMEM],
        out_specs=(VMEM, VMEM),
        scratch_shapes=[pltpu.SemaphoreType.DMA((2 * lists,))],
        compiler_params=PARAMS,
    )(*routes, *sources, near, *far, kv)


def combine_kernel(owner_of, slot_of, stats_ref, out_ref):
    sub = lax.broadcasted_iota(jnp.int32, stats_ref.shape[1:], 0)
    lane = lax.broadcasted_iota(jnp.int32, stats_ref.shape[1:], 1)
    even = sub % 2 == 0
    out_ref[...] = jnp.broadcast_to(jnp.where(even, UNUSED, 0.0)[None], out_ref.shape)
    for block in range(owner_of.shape[0] // 2):
        refs = (2 * block, 2 * block + 1)
        logs, inners = ([], [])
        for ref in refs:
            row = stats_ref[owner_of[ref]]
            row = jnp.where(slot_of[ref] == 0, row, pltpu.roll(row, BLOCK, 1))
            logs.append(row)
            inners.append(pltpu.roll(row, 7, 0))
        top = jnp.maximum(logs[0], logs[1])
        first, second = (jnp.exp(logs[0] - top), jnp.exp(logs[1] - top))
        total = first + second
        joint = (first * inners[0] + second * inners[1]) / total
        both = jnp.where(even, top + jnp.log(total), pltpu.roll(joint, 1, 0))
        both = jnp.where(lane < BLOCK, both, pltpu.roll(both, BLOCK, 1))
        for ref in refs:
            place = owner_of[ref]
            half = jnp.where(lane < BLOCK, 0, 1)
            out_ref[place] = jnp.where(half == slot_of[ref], both, out_ref[place])


def combine(owner_of, slot_of, stats):
    return pl.pallas_call(
        combine_kernel,
        out_shape=jax.ShapeDtypeStruct(stats.shape, jnp.float32),
        in_specs=[SMEM, SMEM, VMEM],
        out_specs=VMEM,
        compiler_params=PARAMS,
    )(owner_of, slot_of, stats)


def score_terms(rows_ref, kv_ref, joint_ref, i, j, passage, head, heads):
    query, grad, key, value = head_views(rows_ref, kv_ref, i, passage, head, heads)
    scores = rows_by_rows(key, query) * SCALE
    prob_grad = rows_by_rows(value, grad)
    probs = jnp.exp(scores - joint_ref[j, 2 * head : 2 * head + 1, :])
    inner = joint_ref[j, 2 * head + 1 : 2 * head + 2, :]
    score_grad = (probs * (prob_grad - inner) * SCALE).astype(jnp.bfloat16)
    return (query, grad, key, probs, score_grad)


def query_kernel(count, lists, local, rows_ref, kv_ref, joint_ref, query_out):
    heads = rows_ref.shape[2] // (2 * HEAD_DIM)
    query_out[...] = jnp.zeros_like(query_out)

    def one_pair(i, second, carry):
        found = []
        for item, head in chains(i, second, heads):
            _, _, key, _, score_grad = score_terms(
                rows_ref, kv_ref, joint_ref, item, lists[item], local[item], head, heads
            )
            query_grad = lax.dot_general(
                score_grad, key, (((0,), (0,)), ((), ())), preferred_element_type=jnp.float32
            )
            found.append((item, head, query_grad.astype(jnp.bfloat16)))
        for item, head, query_grad in found:
            query_out[lists[item], :, pl.ds(head * HEAD_DIM, HEAD_DIM)] = query_grad
        return carry

    over_pairs(count[0], one_pair)


def list_queries(routes, rows, kv, joint):
    return pl.pallas_call(
        query_kernel,
        out_shape=jax.ShapeDtypeStruct(
            (rows.shape[0], rows.shape[1], rows.shape[2] // 2), jnp.bfloat16
        ),
        in_specs=[SMEM] * 3 + [VMEM] * 3,
        out_specs=VMEM,
        compiler_params=PARAMS,
    )(*routes, rows, kv, joint)


def stored_kernel(count, lists, local, rows_ref, kv_ref, joint_ref, stored_out, total):
    heads = rows_ref.shape[2] // (2 * HEAD_DIM)
    width = heads * HEAD_DIM
    total[...] = jnp.zeros_like(total)

    def add_rounded(passage, low, term):
        place = (passage, slice(None), pl.ds(low, HEAD_DIM))
        total[place] += term.astype(jnp.bfloat16).astype(jnp.float32)

    def one_pair(i, second, carry):
        found = []
        for item, head in chains(i, second, heads):
            query, grad, _, probs, score_grad = score_terms(
                rows_ref, kv_ref, joint_ref, item, lists[item], local[item], head, heads
            )
            found.append(
                (
                    head * HEAD_DIM,
                    jnp.dot(score_grad, query, preferred_element_type=jnp.float32),
                    jnp.dot(probs.astype(jnp.bfloat16), grad, preferred_element_type=jnp.float32),
                )
            )
        for low, key_term, value_term in found[:heads]:
            add_rounded(local[i], low, key_term)
            add_rounded(local[i], width + low, value_term)

        @pl.when(second > i)
        def _():
            for low, key_term, value_term in found[heads:]:
                add_rounded(local[second], low, key_term)
                add_rounded(local[second], width + low, value_term)

        return carry

    over_pairs(count[0], one_pair)
    stored_out[...] = total[...].astype(jnp.bfloat16)


def list_stored(routes, rows, kv, joint):
    return pl.pallas_call(
        stored_kernel,
        out_shape=jax.ShapeDtypeStruct(kv.shape, jnp.bfloat16),
        in_specs=[SMEM] * 3 + [VMEM] * 3,
        out_specs=VMEM,
        scratch_shapes=[pltpu.VMEM(kv.shape, jnp.float32)],
        compiler_params=PARAMS,
        cost_estimate=cost(8 * rows.size * HEAD_DIM, 4 * rows.size),
    )(*routes, rows, kv, joint)


def swapped(value):
    return lax.ppermute(value, "section", [(0, 1), (1, 0)])


def turned(value, steps):
    count = lax.axis_size("mp")
    return lax.ppermute(value, "mp", [(i, (i + steps) % count) for i in range(count)])


def exchanged(value):
    return lax.all_to_all(value, "dp", split_axis=0, concat_axis=0, tiled=True)


def along_x(value, steps):
    pairs = [
        (x * Z_CHIPS + z, (x + steps) % X_CHIPS * Z_CHIPS + z)
        for x in range(X_CHIPS)
        for z in range(Z_CHIPS)
    ]
    return lax.ppermute(value, "dp", pairs)


def along_z(value, steps):
    pairs = [
        (x * Z_CHIPS + z, x * Z_CHIPS + (z + steps) % Z_CHIPS)
        for x in range(X_CHIPS)
        for z in range(Z_CHIPS)
    ]
    return lax.ppermute(value, "dp", pairs)


def gathered_in(value, across):
    columns = [[x * Z_CHIPS + z for z in range(Z_CHIPS)] for x in range(X_CHIPS)]
    rows = [[x * Z_CHIPS + z for x in range(X_CHIPS)] for z in range(Z_CHIPS)]
    groups = rows if across else columns
    return lax.all_gather(value, "dp", axis=0, tiled=True, axis_index_groups=groups)


KEY_VALUE = ((True, (0, 1)), (False, (0, 1)))
QUERY_OUT = ((False, (0,)), (True, (1,)))
QUERY = ((False, (0,)), (True, (0,)))


def per_device(tokens, passages, weights, cotangent, neighbours, passage_home, request_lists):
    own_index = lax.axis_index("dp")
    section = lax.axis_index("section")
    group = lax.axis_index("mp")
    groups = lax.axis_size("mp")
    peers = lax.axis_size("dp")
    leading = section == 0
    per_owner, length, width = passages.shape
    half = weights.shape[3] // 2
    row_count = tokens.shape[0]
    block_count = neighbours.shape[0]
    here = jnp.stack([section, group, own_index]).astype(jnp.int32)

    start = jnp.where(leading, tokens, cotangent)
    near_start, far_start = (start[: row_count // 2], start[row_count // 2 :])
    near_parts = [near_start] + [turned(near_start, k) for k in range(1, groups)]
    far_start, near_parts = lax.optimization_barrier((far_start, near_parts))
    far_parts = [far_start] + [turned(far_start, k) for k in range(1, groups)]
    own = weights[0]
    other = swapped(own)

    def own_rows(kept, got):
        return jnp.concatenate(
            [jnp.where(leading, kept, got), jnp.where(leading, got, kept)], axis=1
        )

    def moved(pair):
        return (along_z(pair[0], 1), along_z(pair[1], -1))

    pointers = neighbours.reshape(-1)
    shown = jnp.pad(
        pointers.astype(jnp.bfloat16)[None, :], ((0, 15), (0, 2 * half - pointers.shape[0]))
    )
    kept, sent = project(QUERY_OUT, here, own, other, near_parts)
    near = jnp.concatenate([own_rows(kept, swapped(sent)), shown], axis=0)
    lines = [None] * Z_CHIPS
    lines[0] = near
    step = moved((near, near))
    step, far_parts[1] = lax.optimization_barrier((step, far_parts[1]))
    lines[Z_CHIPS - 1], lines[1] = step
    step = moved(step)
    step, far_parts[2], far_parts[3] = lax.optimization_barrier((step, far_parts[2], far_parts[3]))
    lines[Z_CHIPS - 2], lines[2] = step
    step = moved(step)
    kept, sent = project(QUERY_OUT, here, own, other, far_parts)
    step, kept, sent = lax.optimization_barrier((step, kept, sent))
    lines[Z_CHIPS - 3], lines[3] = step
    cut = near.shape[0] - BLOCK
    last = (along_z(step[0][:cut], 1), along_z(step[1][cut:], -1))
    last, kept, got = lax.optimization_barrier((last, kept, swapped(sent)))
    lines[Z_CHIPS // 2] = jnp.concatenate(last, axis=0)
    far = own_rows(kept, got)
    near = gathered_in(jnp.concatenate(lines, axis=0), True)
    near = near.reshape(peers, row_count // 2 + 16, 2 * half)
    shown = near[:, row_count // 2, : pointers.shape[0]].astype(jnp.int32)

    flat = passages.reshape(per_owner * length, width)
    half_rows = per_owner * length // 2
    held = lax.dynamic_slice_in_dim(flat, section * half_rows, half_rows, 0)
    held, far = lax.optimization_barrier((held, far))
    unit = jnp.stack([far] + [along_x(far, k) for k in range(1, X_CHIPS)])
    units = [None] * (Z_CHIPS + 1)
    units[0] = unit
    ahead, behind = (along_z(unit, 1), along_z(unit, -1))
    held_parts = [held] + [turned(held, k) for k in range(1, groups)]
    ahead, behind, held_parts[1], held_parts[3] = lax.optimization_barrier(
        (ahead, behind, held_parts[1], held_parts[3])
    )
    units[Z_CHIPS - 1], units[1] = (ahead, behind)
    ahead, behind = (along_z(ahead, 1), along_z(behind, -1))
    ahead, behind, held_parts[2] = lax.optimization_barrier((ahead, behind, held_parts[2]))
    units[Z_CHIPS - 2], units[2] = (ahead, behind)
    ahead, behind = (along_z(ahead, 1), along_z(behind, -1))
    kept, sent = project(KEY_VALUE, here, own, other, held_parts)
    ahead, behind, kept, sent = lax.optimization_barrier((ahead, behind, kept, sent))
    units[Z_CHIPS - 3], units[3] = (ahead, behind)
    middle = X_CHIPS // 2
    units[Z_CHIPS // 2] = along_z(ahead[:middle], 1)
    units[Z_CHIPS] = along_z(behind[middle:], -1)
    got = swapped(sent)
    kv = jnp.concatenate(
        [jnp.where(leading, kept, got), jnp.where(leading, got, kept)], axis=0
    ).reshape(per_owner, length, 2 * half)

    tables = routing(here, passage_home, request_lists, shown, per_owner)
    routes, sources, (owner_of, slot_of) = (tables[:3], tables[3:7], tables[7:])
    places = owner_of * 2 + slot_of
    asked, stats = list_stats(routes, sources, near, units, kv)
    joint = exchanged(combine(owner_of, slot_of, exchanged(stats)))
    query_slots = list_queries(routes, asked, kv, joint)
    returned = exchanged(query_slots).reshape(2 * peers, BLOCK, half)
    stored = list_stored(routes, asked, kv, joint)

    def summed(terms):
        total = terms[0].astype(jnp.float32)
        for k in range(1, groups):
            total = total + turned(terms[k], k).astype(jnp.float32)
        return total.astype(jnp.bfloat16)

    stored = stored.reshape(per_owner * length, 2 * half)
    passage_terms = features(KEY_VALUE, here, own, other, stored, swapped(stored))
    passage_grad = summed(passage_terms).reshape(per_owner, length, width // 2)

    terms = jnp.take(returned, places, axis=0, mode="clip").reshape(block_count, 2, BLOCK, half)
    query_grad = (terms[:, 0].astype(jnp.float32) + terms[:, 1].astype(jnp.float32)).astype(
        jnp.bfloat16
    )
    query_grad = query_grad.reshape(row_count, half)
    token_terms = features(QUERY, here, own, other, query_grad, swapped(query_grad))
    return (summed(token_terms), passage_grad)


def solution(mesh):
    in_specs = (
        P("dp", "mp"),
        P("dp", None, "mp"),
        P("section", None, None, "mp"),
        P("dp", "mp"),
        P("dp", None),
        P(),
        P(),
    )
    out_specs = (P("dp", ("section", "mp")), P("dp", None, ("section", "mp")))
    return jax.shard_map(
        per_device, mesh=mesh, in_specs=in_specs, out_specs=out_specs, check_vma=False
    )
```

```python
import math

import jax
import jax.numpy as jnp
from jax import lax
from jax.experimental import pallas as pl
from jax.experimental.pallas import tpu as pltpu
from jax.sharding import PartitionSpec as P

HEAD_DIM = 128
BLOCK = 64
X_CHIPS = 4
Z_CHIPS = 8
SCALE = 1.0 / math.sqrt(HEAD_DIM)
UNUSED = 1e30
VMEM = pl.BlockSpec(memory_space=pltpu.VMEM)
SMEM = pl.BlockSpec(memory_space=pltpu.SMEM)
ANY = pl.BlockSpec(memory_space=pl.ANY)
PARAMS = pltpu.CompilerParams(vmem_limit_bytes=56 * 1024 * 1024)


def cost(flops, moved):
    return pl.CostEstimate(flops=int(flops), bytes_accessed=int(moved), transcendentals=0)


def rows_by_rows(left, right):
    return lax.dot_general(left, right, (((1,), (1,)), ((), ())), preferred_element_type=jnp.float32)


def routing_kernel(
    per_owner, here, home, wanted, shown, count, lists, local, blocks, line, unit, place, owner_of, slot_of
):
    peers, listed = wanted.shape
    refs = shown.shape[1]
    own = here[2]
    lowest = own * per_owner
    own_x, own_z = (lax.div(own, Z_CHIPS), lax.rem(own, Z_CHIPS))

    def one_list(j, found):
        position, held_at = (-1, 0)
        for u in range(listed):
            row = home[wanted[j, u]] - lowest
            hit = (row >= 0) & (row < per_owner)
            position = jnp.where(hit, u, position)
            held_at = jnp.where(hit, row, held_at)

        behind_z = lax.rem(lax.rem(j, Z_CHIPS) - own_z + Z_CHIPS, Z_CHIPS)
        behind_x = lax.rem(own_x - lax.div(j, Z_CHIPS) + X_CHIPS, X_CHIPS)
        row = lax.div(j, Z_CHIPS) * Z_CHIPS + behind_z

        @pl.when(position >= 0)
        def _():
            first, last = (refs - 1, 0)
            for ref in range(refs):
                last = jnp.where(shown[row, ref] == position, ref, last)
                back = refs - 1 - ref
                first = jnp.where(shown[row, back] == position, back, first)
            lists[found] = j
            local[found] = held_at
            blocks[2 * found] = lax.div(first, 2)
            blocks[2 * found + 1] = lax.div(last, 2)
            line[found] = row
            split = (behind_z == Z_CHIPS // 2) & (behind_x >= X_CHIPS // 2)
            unit[found] = jnp.where(split, Z_CHIPS, behind_z)
            place[found] = jnp.where(split, behind_x - X_CHIPS // 2, behind_x)

        return found + jnp.where(position >= 0, 1, 0)

    count[0] = lax.fori_loop(0, peers, one_list, 0)
    for ref in range(refs):
        pointer = shown[own_x * Z_CHIPS, ref]
        owner_of[ref] = lax.div(home[wanted[own, pointer]], per_owner)
        slot = 0
        for before in range(ref):
            slot = jnp.where(shown[own_x * Z_CHIPS, before] == pointer, 1, slot)
        slot_of[ref] = slot


def routing(here, home, wanted, shown, per_owner):
    peers, refs = shown.shape
    sizes = (1, peers, peers, 2 * peers, peers, peers, peers, refs, refs)
    return pl.pallas_call(
        lambda *args: routing_kernel(per_owner, *args),
        out_shape=tuple(jax.ShapeDtypeStruct((size,), jnp.int32) for size in sizes),
        in_specs=[SMEM] * 4,
        out_specs=(SMEM,) * len(sizes),
        compiler_params=PARAMS,
    )(here, home, wanted, shown)


def start_by_section(section, choices, copy_from):
    for which, weights_ref in enumerate(choices):

        @pl.when(section == which)
        def _():
            copy_from(which, weights_ref).start()


def project_kernel(picks, here, own_ref, other_ref, *refs):
    parts = refs[:4]
    keep_ref, send_ref, held, sems = refs[-4:]
    section, group = (here[0], here[1])
    depth = parts[0].shape[1]
    mats = len(picks[0][1])
    half = held.shape[3] // 2

    def fetch(which, source, mat, k):
        low = pl.multiple_of((group - k + 4) % 4 * depth, depth)
        return pltpu.make_async_copy(
            source.at[picks[which][1][mat], pl.ds(low, depth), :],
            held.at[mat, k],
            sems.at[mat * 4 + k],
        )

    for k in range(4):
        for mat in range(mats):
            start_by_section(
                section,
                [own_ref if picks[which][0] else other_ref for which in range(2)],
                lambda which, source: fetch(which, source, mat, k),
            )
    for mat in range(mats):
        total = None
        for k in range(4):
            fetch(0, own_ref, mat, k).wait()
            term = jnp.dot(parts[k][...], held[mat, k], preferred_element_type=jnp.float32)
            total = term if total is None else total + term
        low, high = (total[:, :half].astype(jnp.bfloat16), total[:, half:].astype(jnp.bfloat16))
        columns = pl.ds(mat * half, half)

        @pl.when(section == 0)
        def _():
            keep_ref[:, columns] = low
            send_ref[:, columns] = high

        @pl.when(section == 1)
        def _():
            keep_ref[:, columns] = high
            send_ref[:, columns] = low


def project(picks, here, own, other, parts, after=()):
    rows, depth = parts[0].shape
    mats = len(picks[0][1])
    cols = own.shape[2]
    out = jax.ShapeDtypeStruct((rows, mats * cols // 2), jnp.bfloat16)
    return pl.pallas_call(
        lambda *refs: project_kernel(picks, *refs),
        out_shape=(out, out),
        in_specs=[SMEM, ANY, ANY] + [VMEM] * 4 + [ANY] * len(after),
        out_specs=(VMEM, VMEM),
        scratch_shapes=[
            pltpu.VMEM((mats, 4, depth, cols), jnp.bfloat16),
            pltpu.SemaphoreType.DMA((mats * 4,)),
        ],
        compiler_params=PARAMS,
        cost_estimate=cost(8 * rows * depth * cols * mats, 8 * depth * cols * mats),
    )(here, own, other, *parts, *after)


def features_kernel(picks, here, own_ref, other_ref, mine_ref, got_ref, *refs):
    outs = refs[:4]
    held, sems = refs[4:]
    section, group = (here[0], here[1])
    mats, _, _, chunk, half = held.shape

    def fetch(which, source, mat, side, k):
        low = pl.multiple_of((section * 4 + (group + k) % 4) * chunk, chunk)
        left = which * half if side == 0 else (1 - which) * half
        return pltpu.make_async_copy(
            source.at[picks[which][1][mat], pl.ds(low, chunk), pl.ds(left, half)],
            held.at[mat, side, k],
            sems.at[(mat * 2 + side) * 4 + k],
        )

    order = (2, 1, 3, 0)
    for k in order:
        for mat in range(mats):
            for side in range(2):
                start_by_section(
                    section,
                    [own_ref if picks[which][0] else other_ref for which in range(2)],
                    lambda which, source: fetch(which, source, mat, side, k),
                )
    for k in order:
        total = None
        for mat in range(mats):
            for side, grads in enumerate((mine_ref, got_ref)):
                fetch(0, own_ref, mat, side, k).wait()
                term = rows_by_rows(grads[:, mat * half : (mat + 1) * half], held[mat, side, k])
                total = term if total is None else total + term
        outs[k][...] = total.astype(jnp.bfloat16)


def features(picks, here, own, other, mine, got):
    rows = mine.shape[0]
    mats = len(picks[0][1])
    half = mine.shape[1] // mats
    chunk = own.shape[1] // 8
    out = jax.ShapeDtypeStruct((rows, chunk), jnp.bfloat16)
    return pl.pallas_call(
        lambda *refs: features_kernel(picks, *refs),
        out_shape=(out,) * 4,
        in_specs=[SMEM, ANY, ANY, VMEM, VMEM],
        out_specs=(VMEM,) * 4,
        scratch_shapes=[
            pltpu.VMEM((mats, 2, 4, chunk, half), jnp.bfloat16),
            pltpu.SemaphoreType.DMA((mats * 8,)),
        ],
        compiler_params=PARAMS,
        cost_estimate=cost(16 * rows * chunk * half * mats, 16 * chunk * half * mats),
    )(here, own, other, mine, got)


def head_views(rows_ref, kv_ref, i, passage, head, heads):
    width = heads * HEAD_DIM
    first = pl.ds(head * HEAD_DIM, HEAD_DIM)
    second = pl.ds(width + head * HEAD_DIM, HEAD_DIM)
    return (
        rows_ref[i, :, first],
        rows_ref[i, :, second],
        kv_ref[passage, :, first],
        kv_ref[passage, :, second],
    )


def chains(first, second, heads):
    return [(item, head) for item in (first, second) for head in range(heads)]


def over_pairs(count, body):
    def step(t, carry):
        return body(2 * t, jnp.minimum(2 * t + 1, count - 1), carry)

    lax.fori_loop(0, lax.div(count + 1, 2), step, 0)


def start_all(count, copy_of):
    def step(i, carry):
        copy_of(i).start()
        return carry

    lax.fori_loop(0, count, step, 0)


def wait_all(count, copy_of):
    def step(i, carry):
        copy_of(i).wait()
        return carry

    lax.fori_loop(0, count, step, 0)


def wait_pair(i, second, copy_of):
    copy_of(i).wait()

    @pl.when(second > i)
    def _():
        copy_of(second).wait()


def stats_kernel(count, lists, local, blocks, line, unit, place, near_ref, *refs):
    far_refs = refs[: Z_CHIPS + 1]
    kv_ref, rows_out, out_ref, rows_ref, sems, out_sems = refs[Z_CHIPS + 1 :]
    heads = rows_ref.shape[2] // (2 * HEAD_DIM)
    held = near_ref.shape[1] // BLOCK
    out_ref[...] = jnp.zeros_like(out_ref)

    def fetch(source, first, row, i, slot):
        low = pl.multiple_of(row * BLOCK, BLOCK)
        return pltpu.make_async_copy(
            source.at[first, pl.ds(low, BLOCK), :],
            rows_ref.at[i, pl.ds(slot * BLOCK, BLOCK), :],
            sems.at[2 * i + slot],
        )

    def ask(i, carry):
        for slot in range(2):
            block = blocks[2 * i + slot]

            @pl.when(block < held)
            def _():
                fetch(near_ref, line[i], block, i, slot).start()

            for which, far_ref in enumerate(far_refs):

                @pl.when((block >= held) & (unit[i] == which))
                def _():
                    fetch(far_ref, place[i], block - held, i, slot).start()

        return carry

    lax.fori_loop(0, count[0], ask, 0)

    def keep(i):
        return pltpu.make_async_copy(rows_ref.at[i], rows_out.at[i], out_sems.at[i])

    def arrive(i):
        for slot in range(2):
            fetch(near_ref, 0, 0, i, slot).wait()
        keep(i).start()

    def one_pair(i, second, carry):
        arrive(i)

        @pl.when(second > i)
        def _():
            arrive(second)

        items = chains(i, second, heads)
        parts = [head_views(rows_ref, kv_ref, item, local[item], head, heads) for item, head in items]
        scores = [rows_by_rows(key, query) * SCALE for query, _, key, _ in parts]
        prob_grads = [rows_by_rows(value, grad) for _, grad, _, value in parts]
        tops = [jnp.max(score, axis=0, keepdims=True) for score in scores]
        raised = [jnp.exp(score - top) for score, top in zip(scores, tops)]
        totals = [jnp.sum(part, axis=0, keepdims=True) for part in raised]
        inners = [
            jnp.sum(part * prob_grad, axis=0, keepdims=True) / total
            for part, prob_grad, total in zip(raised, prob_grads, totals)
        ]
        found = [
            (item, head, top + jnp.log(total), inner)
            for (item, head), top, total, inner in zip(items, tops, totals, inners)
        ]
        for item, head, logs, inner in found:
            out_ref[lists[item], 2 * head : 2 * head + 1, :] = logs
            out_ref[lists[item], 2 * head + 1 : 2 * head + 2, :] = inner
        return carry

    over_pairs(count[0], one_pair)
    wait_all(count[0], keep)


def list_stats(routes, sources, near, far, kv):
    lists = routes[1].shape[0]
    return pl.pallas_call(
        stats_kernel,
        out_shape=(
            jax.ShapeDtypeStruct((lists, 2 * BLOCK, near.shape[2]), jnp.bfloat16),
            jax.ShapeDtypeStruct((lists, 8, 2 * BLOCK), jnp.float32),
        ),
        in_specs=[SMEM] * 7 + [ANY] * (Z_CHIPS + 2) + [VMEM],
        out_specs=(ANY, VMEM),
        scratch_shapes=[
            pltpu.VMEM((lists, 2 * BLOCK, near.shape[2]), jnp.bfloat16),
            pltpu.SemaphoreType.DMA((2 * lists,)),
            pltpu.SemaphoreType.DMA((lists,)),
        ],
        compiler_params=PARAMS,
    )(*routes, *sources, near, *far, kv)


def combine_kernel(owner_of, slot_of, stats_ref, out_ref):
    sub = lax.broadcasted_iota(jnp.int32, stats_ref.shape[1:], 0)
    lane = lax.broadcasted_iota(jnp.int32, stats_ref.shape[1:], 1)
    even = sub % 2 == 0
    out_ref[...] = jnp.broadcast_to(jnp.where(even, UNUSED, 0.0)[None], out_ref.shape)
    for block in range(owner_of.shape[0] // 2):
        refs = (2 * block, 2 * block + 1)
        logs, inners = ([], [])
        for ref in refs:
            row = stats_ref[owner_of[ref]]
            row = jnp.where(slot_of[ref] == 0, row, pltpu.roll(row, BLOCK, 1))
            logs.append(row)
            inners.append(pltpu.roll(row, 7, 0))
        top = jnp.maximum(logs[0], logs[1])
        first, second = (jnp.exp(logs[0] - top), jnp.exp(logs[1] - top))
        total = first + second
        joint = (first * inners[0] + second * inners[1]) / total
        both = jnp.where(even, top + jnp.log(total), pltpu.roll(joint, 1, 0))
        both = jnp.where(lane < BLOCK, both, pltpu.roll(both, BLOCK, 1))
        for ref in refs:
            place = owner_of[ref]
            half = jnp.where(lane < BLOCK, 0, 1)
            out_ref[place] = jnp.where(half == slot_of[ref], both, out_ref[place])


def combine(owner_of, slot_of, stats):
    return pl.pallas_call(
        combine_kernel,
        out_shape=jax.ShapeDtypeStruct(stats.shape, jnp.float32),
        in_specs=[SMEM, SMEM, VMEM],
        out_specs=VMEM,
        compiler_params=PARAMS,
    )(owner_of, slot_of, stats)


def score_terms(rows_ref, kv_ref, joint_ref, lists, local, items, heads):
    parts = [head_views(rows_ref, kv_ref, i, local[i], head, heads) for i, head in items]
    scores = [rows_by_rows(key, query) for query, _, key, _ in parts]
    prob_grads = [rows_by_rows(value, grad) for _, grad, _, value in parts]
    logs = [joint_ref[lists[i], 2 * head : 2 * head + 1, :] for i, head in items]
    inners = [joint_ref[lists[i], 2 * head + 1 : 2 * head + 2, :] for i, head in items]
    probs = [jnp.exp(score * SCALE - log) for score, log in zip(scores, logs)]
    score_grads = [
        (prob * (prob_grad - inner) * SCALE).astype(jnp.bfloat16)
        for prob, prob_grad, inner in zip(probs, prob_grads, inners)
    ]
    return (parts, probs, score_grads)


def query_kernel(
    count, lists, local, rows_in, kv_ref, joint_ref, query_out, rows_ref, held, sems, out_sems
):
    heads = rows_ref.shape[2] // (2 * HEAD_DIM)

    def fetch(i):
        return pltpu.make_async_copy(rows_in.at[i], rows_ref.at[i], sems.at[i])

    def give(i):
        return pltpu.make_async_copy(held.at[i], query_out.at[lists[i]], out_sems.at[i])

    start_all(count[0], fetch)

    def one_pair(i, second, carry):
        wait_pair(i, second, fetch)
        items = chains(i, second, heads)
        parts, _, score_grads = score_terms(
            rows_ref, kv_ref, joint_ref, lists, local, items, heads
        )
        query_grads = [
            lax.dot_general(
                score_grad, part[2], (((0,), (0,)), ((), ())), preferred_element_type=jnp.float32
            )
            for score_grad, part in zip(score_grads, parts)
        ]
        for (item, head), query_grad in zip(items, query_grads):
            held[item, :, pl.ds(head * HEAD_DIM, HEAD_DIM)] = query_grad.astype(jnp.bfloat16)
        give(i).start()

        @pl.when(second > i)
        def _():
            give(second).start()

        return carry

    over_pairs(count[0], one_pair)
    wait_all(count[0], give)


def list_queries(routes, rows, kv, joint):
    lists, depth, width = rows.shape
    return pl.pallas_call(
        query_kernel,
        out_shape=jax.ShapeDtypeStruct((lists, depth, width // 2), jnp.bfloat16),
        in_specs=[SMEM] * 3 + [ANY, VMEM, VMEM],
        out_specs=ANY,
        scratch_shapes=[
            pltpu.VMEM(rows.shape, jnp.bfloat16),
            pltpu.VMEM((lists, depth, width // 2), jnp.bfloat16),
            pltpu.SemaphoreType.DMA((lists,)),
            pltpu.SemaphoreType.DMA((lists,)),
        ],
        compiler_params=PARAMS,
    )(*routes, rows, kv, joint)


def stored_kernel(
    count, lists, local, rows_in, kv_ref, joint_ref, stored_out, total, rows_ref, sems
):
    heads = rows_ref.shape[2] // (2 * HEAD_DIM)
    width = heads * HEAD_DIM

    def fetch(i):
        return pltpu.make_async_copy(rows_in.at[i], rows_ref.at[i], sems.at[i])

    start_all(count[0], fetch)
    total[...] = jnp.zeros_like(total)

    def add_rounded(passage, low, term):
        place = (passage, slice(None), pl.ds(low, HEAD_DIM))
        total[place] += term.astype(jnp.bfloat16).astype(jnp.float32)

    def one_pair(i, second, carry):
        wait_pair(i, second, fetch)
        items = chains(i, second, heads)
        parts, probs, score_grads = score_terms(
            rows_ref, kv_ref, joint_ref, lists, local, items, heads
        )
        found = [
            (
                head * HEAD_DIM,
                jnp.dot(score_grad, part[0], preferred_element_type=jnp.float32),
                jnp.dot(prob.astype(jnp.bfloat16), part[1], preferred_element_type=jnp.float32),
            )
            for (_, head), part, prob, score_grad in zip(items, parts, probs, score_grads)
        ]
        for low, key_term, value_term in found[:heads]:
            add_rounded(local[i], low, key_term)
            add_rounded(local[i], width + low, value_term)

        @pl.when(second > i)
        def _():
            for low, key_term, value_term in found[heads:]:
                add_rounded(local[second], low, key_term)
                add_rounded(local[second], width + low, value_term)

        return carry

    over_pairs(count[0], one_pair)
    stored_out[...] = total[...].astype(jnp.bfloat16)


def list_stored(routes, rows, kv, joint):
    return pl.pallas_call(
        stored_kernel,
        out_shape=jax.ShapeDtypeStruct(kv.shape, jnp.bfloat16),
        in_specs=[SMEM] * 3 + [ANY, VMEM, VMEM],
        out_specs=VMEM,
        scratch_shapes=[
            pltpu.VMEM(kv.shape, jnp.float32),
            pltpu.VMEM(rows.shape, jnp.bfloat16),
            pltpu.SemaphoreType.DMA((rows.shape[0],)),
        ],
        compiler_params=PARAMS,
        cost_estimate=cost(8 * rows.size * HEAD_DIM, 4 * rows.size),
    )(*routes, rows, kv, joint)


def swapped(value):
    return lax.ppermute(value, "section", [(0, 1), (1, 0)])


def turned(value, steps):
    count = lax.axis_size("mp")
    return lax.ppermute(value, "mp", [(i, (i + steps) % count) for i in range(count)])


def exchanged(value):
    return lax.all_to_all(value, "dp", split_axis=0, concat_axis=0, tiled=True)


def along_x(value, steps):
    pairs = [
        (x * Z_CHIPS + z, (x + steps) % X_CHIPS * Z_CHIPS + z)
        for x in range(X_CHIPS)
        for z in range(Z_CHIPS)
    ]
    return lax.ppermute(value, "dp", pairs)


def along_z(value, steps):
    pairs = [
        (x * Z_CHIPS + z, x * Z_CHIPS + (z + steps) % Z_CHIPS)
        for x in range(X_CHIPS)
        for z in range(Z_CHIPS)
    ]
    return lax.ppermute(value, "dp", pairs)


def gathered_in(value, across):
    columns = [[x * Z_CHIPS + z for z in range(Z_CHIPS)] for x in range(X_CHIPS)]
    rows = [[x * Z_CHIPS + z for x in range(X_CHIPS)] for z in range(Z_CHIPS)]
    groups = rows if across else columns
    return lax.all_gather(value, "dp", axis=0, tiled=True, axis_index_groups=groups)


KEY_VALUE = ((True, (0, 1)), (False, (0, 1)))
QUERY_OUT = ((False, (0,)), (True, (1,)))
QUERY = ((False, (0,)), (True, (0,)))


def per_device(tokens, passages, weights, cotangent, neighbours, passage_home, request_lists):
    own_index = lax.axis_index("dp")
    section = lax.axis_index("section")
    group = lax.axis_index("mp")
    groups = lax.axis_size("mp")
    peers = lax.axis_size("dp")
    leading = section == 0
    per_owner, length, width = passages.shape
    half = weights.shape[3] // 2
    row_count = tokens.shape[0]
    block_count = neighbours.shape[0]
    here = jnp.stack([section, group, own_index]).astype(jnp.int32)

    start = jnp.where(leading, tokens, cotangent)
    near_start, far_start = (start[: row_count // 2], start[row_count // 2 :])
    near_parts = [near_start] + [turned(near_start, k) for k in range(1, groups)]
    far_start, near_parts = lax.optimization_barrier((far_start, near_parts))
    far_parts = [far_start] + [turned(far_start, k) for k in range(1, groups)]
    own = weights[0]
    other = swapped(own)

    def own_rows(kept, got):
        return jnp.concatenate(
            [jnp.where(leading, kept, got), jnp.where(leading, got, kept)], axis=1
        )

    def moved(pair):
        return (along_z(pair[0], 1), along_z(pair[1], -1))

    pointers = neighbours.reshape(-1)
    shown = jnp.pad(
        pointers.astype(jnp.bfloat16)[None, :], ((0, 15), (0, 2 * half - pointers.shape[0]))
    )
    kept, sent = project(QUERY_OUT, here, own, other, near_parts)
    near = jnp.concatenate([own_rows(kept, swapped(sent)), shown], axis=0)
    lines = [None] * Z_CHIPS
    lines[0] = near
    step = moved((near, near))
    step, far_parts[1] = lax.optimization_barrier((step, far_parts[1]))
    lines[Z_CHIPS - 1], lines[1] = step
    step = moved(step)
    step, far_parts[2], far_parts[3] = lax.optimization_barrier((step, far_parts[2], far_parts[3]))
    lines[Z_CHIPS - 2], lines[2] = step
    step = moved(step)
    kept, sent = project(QUERY_OUT, here, own, other, far_parts)
    step, kept, sent = lax.optimization_barrier((step, kept, sent))
    lines[Z_CHIPS - 3], lines[3] = step
    cut = near.shape[0] - BLOCK
    last = (along_z(step[0][:cut], 1), along_z(step[1][cut:], -1))
    last, kept, got = lax.optimization_barrier((last, kept, swapped(sent)))
    lines[Z_CHIPS // 2] = jnp.concatenate(last, axis=0)
    far = own_rows(kept, got)
    near = gathered_in(jnp.concatenate(lines, axis=0), True)
    near = near.reshape(peers, row_count // 2 + 16, 2 * half)
    shown = near[:, row_count // 2, : pointers.shape[0]].astype(jnp.int32)

    flat = passages.reshape(per_owner * length, width)
    half_rows = per_owner * length // 2
    held = lax.dynamic_slice_in_dim(flat, section * half_rows, half_rows, 0)
    held, far = lax.optimization_barrier((held, far))
    unit = jnp.stack([far] + [along_x(far, k) for k in range(1, X_CHIPS)])
    units = [None] * (Z_CHIPS + 1)
    units[0] = unit
    ahead, behind = (along_z(unit, 1), along_z(unit, -1))
    held_parts = [held] + [turned(held, k) for k in range(1, groups)]
    ahead, behind, held_parts[1], held_parts[3] = lax.optimization_barrier(
        (ahead, behind, held_parts[1], held_parts[3])
    )
    units[Z_CHIPS - 1], units[1] = (ahead, behind)
    ahead, behind = (along_z(ahead, 1), along_z(behind, -1))
    ahead, behind, held_parts[2] = lax.optimization_barrier((ahead, behind, held_parts[2]))
    units[Z_CHIPS - 2], units[2] = (ahead, behind)
    ahead, behind = (along_z(ahead, 1), along_z(behind, -1))
    kept, sent = project(KEY_VALUE, here, own, other, held_parts)
    ahead, behind, kept, sent = lax.optimization_barrier((ahead, behind, kept, sent))
    units[Z_CHIPS - 3], units[3] = (ahead, behind)
    middle = X_CHIPS // 2
    units[Z_CHIPS // 2] = along_z(ahead[:middle], 1)
    units[Z_CHIPS] = along_z(behind[middle:], -1)
    got = swapped(sent)
    kv = jnp.concatenate(
        [jnp.where(leading, kept, got), jnp.where(leading, got, kept)], axis=0
    ).reshape(per_owner, length, 2 * half)

    tables = routing(here, passage_home, request_lists, shown, per_owner)
    routes, sources, (owner_of, slot_of) = (tables[:3], tables[3:7], tables[7:])
    places = owner_of * 2 + slot_of
    asked, stats = list_stats(routes, sources, near, units, kv)
    joint = exchanged(combine(owner_of, slot_of, exchanged(stats)))
    query_slots = list_queries(routes, asked, kv, joint)
    returned = exchanged(query_slots).reshape(2 * peers, BLOCK, half)
    stored = list_stored(routes, asked, kv, joint)

    def summed(terms):
        total = terms[0].astype(jnp.float32)
        for k in range(1, groups):
            total = total + turned(terms[k], k).astype(jnp.float32)
        return total.astype(jnp.bfloat16)

    stored = stored.reshape(per_owner * length, 2 * half)
    passage_terms = features(KEY_VALUE, here, own, other, stored, swapped(stored))
    passage_grad = summed(passage_terms).reshape(per_owner, length, width // 2)

    terms = jnp.take(returned, places, axis=0, mode="clip").reshape(block_count, 2, BLOCK, half)
    query_grad = (terms[:, 0].astype(jnp.float32) + terms[:, 1].astype(jnp.float32)).astype(
        jnp.bfloat16
    )
    query_grad = query_grad.reshape(row_count, half)
    token_terms = features(QUERY, here, own, other, query_grad, swapped(query_grad))
    return (summed(token_terms), passage_grad)


def solution(mesh):
    in_specs = (
        P("dp", "mp"),
        P("dp", None, "mp"),
        P("section", None, None, "mp"),
        P("dp", "mp"),
        P("dp", None),
        P(),
        P(),
    )
    out_specs = (P("dp", ("section", "mp")), P("dp", None, ("section", "mp")))
    return jax.shard_map(
        per_device, mesh=mesh, in_specs=in_specs, out_specs=out_specs, check_vma=False
    )
```

```python
import math

import jax
import jax.numpy as jnp
from jax import lax
from jax.experimental import pallas as pl
from jax.experimental.pallas import tpu as pltpu
from jax.sharding import PartitionSpec as P

HEAD_DIM = 128
BLOCK = 64
X_CHIPS = 4
Z_CHIPS = 8
SCALE = 1.0 / math.sqrt(HEAD_DIM)
UNUSED = 1e30
VMEM = pl.BlockSpec(memory_space=pltpu.VMEM)
SMEM = pl.BlockSpec(memory_space=pltpu.SMEM)
ANY = pl.BlockSpec(memory_space=pl.ANY)
PARAMS = pltpu.CompilerParams(vmem_limit_bytes=56 * 1024 * 1024)


def cost(flops, moved):
    return pl.CostEstimate(flops=int(flops), bytes_accessed=int(moved), transcendentals=0)


def rows_by_rows(left, right):
    return lax.dot_general(left, right, (((1,), (1,)), ((), ())), preferred_element_type=jnp.float32)


def lists_kernel(
    per_owner, here, home, wanted, count, lists, local, spots, unit, place, owners
):
    peers, listed = wanted.shape
    own = here[2]
    lowest = own * per_owner
    own_x, own_z = (lax.div(own, Z_CHIPS), lax.rem(own, Z_CHIPS))

    def one_list(j, found):
        position, held_at = (-1, 0)
        for u in range(listed):
            row = home[wanted[j, u]] - lowest
            hit = (row >= 0) & (row < per_owner)
            position = jnp.where(hit, u, position)
            held_at = jnp.where(hit, row, held_at)
        behind_z = lax.rem(lax.rem(j, Z_CHIPS) - own_z + Z_CHIPS, Z_CHIPS)
        behind_x = lax.rem(own_x - lax.div(j, Z_CHIPS) + X_CHIPS, X_CHIPS)

        @pl.when(position >= 0)
        def _():
            lists[found] = j
            local[found] = held_at
            spots[2 * found] = position
            spots[2 * found + 1] = lax.div(j, Z_CHIPS) * Z_CHIPS + behind_z
            split = (behind_z == Z_CHIPS // 2) & (behind_x >= X_CHIPS // 2)
            unit[found] = jnp.where(split, Z_CHIPS, behind_z)
            place[found] = jnp.where(split, behind_x - X_CHIPS // 2, behind_x)

        return found + jnp.where(position >= 0, 1, 0)

    count[0] = lax.fori_loop(0, peers, one_list, 0)
    for u in range(listed):
        owners[u] = lax.div(home[wanted[own, u]], per_owner)


def blocks_kernel(here, count, spots, owners, shown, blocks, line, owner_of, slot_of):
    refs = shown.shape[1]
    own_row = lax.div(here[2], Z_CHIPS) * Z_CHIPS

    def one_list(i, carry):
        position, row = (spots[2 * i], spots[2 * i + 1])
        first, last = (refs - 1, 0)
        for ref in range(refs):
            last = jnp.where(shown[row, ref] == position, ref, last)
            back = refs - 1 - ref
            first = jnp.where(shown[row, back] == position, back, first)
        blocks[2 * i] = lax.div(first, 2)
        blocks[2 * i + 1] = lax.div(last, 2)
        line[i] = row
        return carry

    lax.fori_loop(0, count[0], one_list, 0)
    for ref in range(refs):
        pointer = shown[own_row, ref]
        owner_of[ref] = owners[pointer]
        slot = 0
        for before in range(ref):
            slot = jnp.where(shown[own_row, before] == pointer, 1, slot)
        slot_of[ref] = slot


def integers(kernel, sizes, *args):
    return pl.pallas_call(
        kernel,
        out_shape=tuple(jax.ShapeDtypeStruct((size,), jnp.int32) for size in sizes),
        in_specs=[SMEM] * len(args),
        out_specs=(SMEM,) * len(sizes),
        compiler_params=PARAMS,
    )(*args)


def start_by_section(section, choices, copy_from):
    for which, weights_ref in enumerate(choices):

        @pl.when(section == which)
        def _():
            copy_from(which, weights_ref).start()


def project_kernel(picks, here, own_ref, other_ref, *refs):
    parts = refs[:4]
    keep_ref, send_ref, held, sems = refs[-4:]
    section, group = (here[0], here[1])
    depth = parts[0].shape[1]
    mats = len(picks[0][1])
    half = held.shape[3] // 2

    def fetch(which, source, mat, k):
        low = pl.multiple_of((group - k + 4) % 4 * depth, depth)
        return pltpu.make_async_copy(
            source.at[picks[which][1][mat], pl.ds(low, depth), :],
            held.at[mat, k],
            sems.at[mat * 4 + k],
        )

    for k in range(4):
        for mat in range(mats):
            start_by_section(
                section,
                [own_ref if picks[which][0] else other_ref for which in range(2)],
                lambda which, source: fetch(which, source, mat, k),
            )
    for mat in range(mats):
        total = None
        for k in range(4):
            fetch(0, own_ref, mat, k).wait()
            term = jnp.dot(parts[k][...], held[mat, k], preferred_element_type=jnp.float32)
            total = term if total is None else total + term
        low, high = (total[:, :half].astype(jnp.bfloat16), total[:, half:].astype(jnp.bfloat16))
        columns = pl.ds(mat * half, half)

        @pl.when(section == 0)
        def _():
            keep_ref[:, columns] = low
            send_ref[:, columns] = high

        @pl.when(section == 1)
        def _():
            keep_ref[:, columns] = high
            send_ref[:, columns] = low


def project(picks, here, own, other, parts, after=()):
    rows, depth = parts[0].shape
    mats = len(picks[0][1])
    cols = own.shape[2]
    out = jax.ShapeDtypeStruct((rows, mats * cols // 2), jnp.bfloat16)
    return pl.pallas_call(
        lambda *refs: project_kernel(picks, *refs),
        out_shape=(out, out),
        in_specs=[SMEM, ANY, ANY] + [VMEM] * 4 + [ANY] * len(after),
        out_specs=(VMEM, VMEM),
        scratch_shapes=[
            pltpu.VMEM((mats, 4, depth, cols), jnp.bfloat16),
            pltpu.SemaphoreType.DMA((mats * 4,)),
        ],
        compiler_params=PARAMS,
        cost_estimate=cost(8 * rows * depth * cols * mats, 8 * depth * cols * mats),
    )(here, own, other, *parts, *after)


def features_kernel(picks, here, own_ref, other_ref, mine_ref, got_ref, *refs):
    outs = refs[:4]
    held, sems = refs[4:]
    section, group = (here[0], here[1])
    mats, _, _, chunk, half = held.shape

    def fetch(which, source, mat, side, k):
        low = pl.multiple_of((section * 4 + (group + k) % 4) * chunk, chunk)
        left = which * half if side == 0 else (1 - which) * half
        return pltpu.make_async_copy(
            source.at[picks[which][1][mat], pl.ds(low, chunk), pl.ds(left, half)],
            held.at[mat, side, k],
            sems.at[(mat * 2 + side) * 4 + k],
        )

    order = (2, 1, 3, 0)
    for k in order:
        for mat in range(mats):
            for side in range(2):
                start_by_section(
                    section,
                    [own_ref if picks[which][0] else other_ref for which in range(2)],
                    lambda which, source: fetch(which, source, mat, side, k),
                )
    for k in order:
        total = None
        for mat in range(mats):
            for side, grads in enumerate((mine_ref, got_ref)):
                fetch(0, own_ref, mat, side, k).wait()
                term = rows_by_rows(grads[:, mat * half : (mat + 1) * half], held[mat, side, k])
                total = term if total is None else total + term
        outs[k][...] = total.astype(jnp.bfloat16)


def features(picks, here, own, other, mine, got):
    rows = mine.shape[0]
    mats = len(picks[0][1])
    half = mine.shape[1] // mats
    chunk = own.shape[1] // 8
    out = jax.ShapeDtypeStruct((rows, chunk), jnp.bfloat16)
    return pl.pallas_call(
        lambda *refs: features_kernel(picks, *refs),
        out_shape=(out,) * 4,
        in_specs=[SMEM, ANY, ANY, VMEM, VMEM],
        out_specs=(VMEM,) * 4,
        scratch_shapes=[
            pltpu.VMEM((mats, 2, 4, chunk, half), jnp.bfloat16),
            pltpu.SemaphoreType.DMA((mats * 8,)),
        ],
        compiler_params=PARAMS,
        cost_estimate=cost(16 * rows * chunk * half * mats, 16 * chunk * half * mats),
    )(here, own, other, mine, got)


def head_views(rows_ref, kv_ref, i, passage, head, heads):
    width = heads * HEAD_DIM
    first = pl.ds(head * HEAD_DIM, HEAD_DIM)
    second = pl.ds(width + head * HEAD_DIM, HEAD_DIM)
    return (
        rows_ref[i, :, first],
        rows_ref[i, :, second],
        kv_ref[passage, :, first],
        kv_ref[passage, :, second],
    )


def chains(first, second, heads):
    return [(item, head) for item in (first, second) for head in range(heads)]


def over_pairs(count, body):
    def step(t, carry):
        return body(2 * t, jnp.minimum(2 * t + 1, count - 1), carry)

    lax.fori_loop(0, lax.div(count + 1, 2), step, 0)


def start_all(count, copy_of):
    def step(i, carry):
        copy_of(i).start()
        return carry

    lax.fori_loop(0, count, step, 0)


def wait_all(count, copy_of):
    def step(i, carry):
        copy_of(i).wait()
        return carry

    lax.fori_loop(0, count, step, 0)


def wait_pair(i, second, copy_of):
    copy_of(i).wait()

    @pl.when(second > i)
    def _():
        copy_of(second).wait()


def stats_kernel(count, lists, local, blocks, line, unit, place, near_ref, *refs):
    far_refs = refs[: Z_CHIPS + 1]
    kv_ref, rows_out, out_ref, rows_ref, sems, out_sems = refs[Z_CHIPS + 1 :]
    heads = rows_ref.shape[2] // (2 * HEAD_DIM)
    held = near_ref.shape[1] // BLOCK
    out_ref[...] = jnp.zeros_like(out_ref)

    def fetch(source, first, row, i, slot):
        low = pl.multiple_of(row * BLOCK, BLOCK)
        return pltpu.make_async_copy(
            source.at[first, pl.ds(low, BLOCK), :],
            rows_ref.at[i, pl.ds(slot * BLOCK, BLOCK), :],
            sems.at[2 * i + slot],
        )

    def ask(i, carry):
        for slot in range(2):
            block = blocks[2 * i + slot]

            @pl.when(block < held)
            def _():
                fetch(near_ref, line[i], block, i, slot).start()

            for which, far_ref in enumerate(far_refs):

                @pl.when((block >= held) & (unit[i] == which))
                def _():
                    fetch(far_ref, place[i], block - held, i, slot).start()

        return carry

    lax.fori_loop(0, count[0], ask, 0)

    def keep(i):
        return pltpu.make_async_copy(rows_ref.at[i], rows_out.at[i], out_sems.at[i])

    def arrive(i):
        for slot in range(2):
            fetch(near_ref, 0, 0, i, slot).wait()
        keep(i).start()

    def one_pair(i, second, carry):
        arrive(i)

        @pl.when(second > i)
        def _():
            arrive(second)

        items = chains(i, second, heads)
        parts = [head_views(rows_ref, kv_ref, item, local[item], head, heads) for item, head in items]
        scores = [rows_by_rows(key, query) * SCALE for query, _, key, _ in parts]
        prob_grads = [rows_by_rows(value, grad) for _, grad, _, value in parts]
        tops = [jnp.max(score, axis=0, keepdims=True) for score in scores]
        raised = [jnp.exp(score - top) for score, top in zip(scores, tops)]
        totals = [jnp.sum(part, axis=0, keepdims=True) for part in raised]
        inners = [
            jnp.sum(part * prob_grad, axis=0, keepdims=True) / total
            for part, prob_grad, total in zip(raised, prob_grads, totals)
        ]
        found = [
            (item, head, top + jnp.log(total), inner)
            for (item, head), top, total, inner in zip(items, tops, totals, inners)
        ]
        for item, head, logs, inner in found:
            out_ref[lists[item], 2 * head : 2 * head + 1, :] = logs
            out_ref[lists[item], 2 * head + 1 : 2 * head + 2, :] = inner
        return carry

    over_pairs(count[0], one_pair)
    wait_all(count[0], keep)


def list_stats(routes, sources, near, far, kv):
    lists = routes[1].shape[0]
    return pl.pallas_call(
        stats_kernel,
        out_shape=(
            jax.ShapeDtypeStruct((lists, 2 * BLOCK, near.shape[2]), jnp.bfloat16),
            jax.ShapeDtypeStruct((lists, 8, 2 * BLOCK), jnp.float32),
        ),
        in_specs=[SMEM] * 7 + [ANY] * (Z_CHIPS + 2) + [VMEM],
        out_specs=(ANY, VMEM),
        scratch_shapes=[
            pltpu.VMEM((lists, 2 * BLOCK, near.shape[2]), jnp.bfloat16),
            pltpu.SemaphoreType.DMA((2 * lists,)),
            pltpu.SemaphoreType.DMA((lists,)),
        ],
        compiler_params=PARAMS,
    )(*routes, *sources, near, *far, kv)


def combine_kernel(owner_of, slot_of, stats_ref, out_ref):
    sub = lax.broadcasted_iota(jnp.int32, stats_ref.shape[1:], 0)
    lane = lax.broadcasted_iota(jnp.int32, stats_ref.shape[1:], 1)
    even = sub % 2 == 0
    out_ref[...] = jnp.broadcast_to(jnp.where(even, UNUSED, 0.0)[None], out_ref.shape)
    for block in range(owner_of.shape[0] // 2):
        refs = (2 * block, 2 * block + 1)
        logs, inners = ([], [])
        for ref in refs:
            row = stats_ref[owner_of[ref]]
            row = jnp.where(slot_of[ref] == 0, row, pltpu.roll(row, BLOCK, 1))
            logs.append(row)
            inners.append(pltpu.roll(row, 7, 0))
        top = jnp.maximum(logs[0], logs[1])
        first, second = (jnp.exp(logs[0] - top), jnp.exp(logs[1] - top))
        total = first + second
        joint = (first * inners[0] + second * inners[1]) / total
        both = jnp.where(even, top + jnp.log(total), pltpu.roll(joint, 1, 0))
        both = jnp.where(lane < BLOCK, both, pltpu.roll(both, BLOCK, 1))
        for ref in refs:
            place = owner_of[ref]
            half = jnp.where(lane < BLOCK, 0, 1)
            out_ref[place] = jnp.where(half == slot_of[ref], both, out_ref[place])


def combine(owner_of, slot_of, stats):
    return pl.pallas_call(
        combine_kernel,
        out_shape=jax.ShapeDtypeStruct(stats.shape, jnp.float32),
        in_specs=[SMEM, SMEM, VMEM],
        out_specs=VMEM,
        compiler_params=PARAMS,
    )(owner_of, slot_of, stats)


def score_terms(rows_ref, kv_ref, joint_ref, lists, local, items, heads):
    parts = [head_views(rows_ref, kv_ref, i, local[i], head, heads) for i, head in items]
    scores = [rows_by_rows(key, query) for query, _, key, _ in parts]
    prob_grads = [rows_by_rows(value, grad) for _, grad, _, value in parts]
    logs = [joint_ref[lists[i], 2 * head : 2 * head + 1, :] for i, head in items]
    inners = [joint_ref[lists[i], 2 * head + 1 : 2 * head + 2, :] for i, head in items]
    probs = [jnp.exp(score * SCALE - log) for score, log in zip(scores, logs)]
    score_grads = [
        (prob * (prob_grad - inner) * SCALE).astype(jnp.bfloat16)
        for prob, prob_grad, inner in zip(probs, prob_grads, inners)
    ]
    return (parts, probs, score_grads)


def query_kernel(
    count, lists, local, rows_in, kv_ref, joint_ref, query_out, rows_ref, held, sems, out_sems
):
    heads = rows_ref.shape[2] // (2 * HEAD_DIM)

    def fetch(i):
        return pltpu.make_async_copy(rows_in.at[i], rows_ref.at[i], sems.at[i])

    def give(i):
        return pltpu.make_async_copy(held.at[i], query_out.at[lists[i]], out_sems.at[i])

    start_all(count[0], fetch)

    def one_pair(i, second, carry):
        wait_pair(i, second, fetch)
        items = chains(i, second, heads)
        parts, _, score_grads = score_terms(
            rows_ref, kv_ref, joint_ref, lists, local, items, heads
        )
        query_grads = [
            lax.dot_general(
                score_grad, part[2], (((0,), (0,)), ((), ())), preferred_element_type=jnp.float32
            )
            for score_grad, part in zip(score_grads, parts)
        ]
        for (item, head), query_grad in zip(items, query_grads):
            held[item, :, pl.ds(head * HEAD_DIM, HEAD_DIM)] = query_grad.astype(jnp.bfloat16)
        give(i).start()

        @pl.when(second > i)
        def _():
            give(second).start()

        return carry

    over_pairs(count[0], one_pair)
    wait_all(count[0], give)


def list_queries(routes, rows, kv, joint):
    lists, depth, width = rows.shape
    return pl.pallas_call(
        query_kernel,
        out_shape=jax.ShapeDtypeStruct((lists, depth, width // 2), jnp.bfloat16),
        in_specs=[SMEM] * 3 + [ANY, VMEM, VMEM],
        out_specs=ANY,
        scratch_shapes=[
            pltpu.VMEM(rows.shape, jnp.bfloat16),
            pltpu.VMEM((lists, depth, width // 2), jnp.bfloat16),
            pltpu.SemaphoreType.DMA((lists,)),
            pltpu.SemaphoreType.DMA((lists,)),
        ],
        compiler_params=PARAMS,
    )(*routes, rows, kv, joint)


def stored_kernel(
    count, lists, local, rows_in, kv_ref, joint_ref, stored_out, total, rows_ref, sems
):
    heads = rows_ref.shape[2] // (2 * HEAD_DIM)
    width = heads * HEAD_DIM

    def fetch(i):
        return pltpu.make_async_copy(rows_in.at[i], rows_ref.at[i], sems.at[i])

    start_all(count[0], fetch)
    total[...] = jnp.zeros_like(total)

    def add_rounded(passage, low, term):
        place = (passage, slice(None), pl.ds(low, HEAD_DIM))
        total[place] += term.astype(jnp.bfloat16).astype(jnp.float32)

    def one_pair(i, second, carry):
        wait_pair(i, second, fetch)
        items = chains(i, second, heads)
        parts, probs, score_grads = score_terms(
            rows_ref, kv_ref, joint_ref, lists, local, items, heads
        )
        found = [
            (
                head * HEAD_DIM,
                jnp.dot(score_grad, part[0], preferred_element_type=jnp.float32),
                jnp.dot(prob.astype(jnp.bfloat16), part[1], preferred_element_type=jnp.float32),
            )
            for (_, head), part, prob, score_grad in zip(items, parts, probs, score_grads)
        ]
        for low, key_term, value_term in found[:heads]:
            add_rounded(local[i], low, key_term)
            add_rounded(local[i], width + low, value_term)

        @pl.when(second > i)
        def _():
            for low, key_term, value_term in found[heads:]:
                add_rounded(local[second], low, key_term)
                add_rounded(local[second], width + low, value_term)

        return carry

    over_pairs(count[0], one_pair)
    stored_out[...] = total[...].astype(jnp.bfloat16)


def list_stored(routes, rows, kv, joint):
    return pl.pallas_call(
        stored_kernel,
        out_shape=jax.ShapeDtypeStruct(kv.shape, jnp.bfloat16),
        in_specs=[SMEM] * 3 + [ANY, VMEM, VMEM],
        out_specs=VMEM,
        scratch_shapes=[
            pltpu.VMEM(kv.shape, jnp.float32),
            pltpu.VMEM(rows.shape, jnp.bfloat16),
            pltpu.SemaphoreType.DMA((rows.shape[0],)),
        ],
        compiler_params=PARAMS,
        cost_estimate=cost(8 * rows.size * HEAD_DIM, 4 * rows.size),
    )(*routes, rows, kv, joint)


def swapped(value):
    return lax.ppermute(value, "section", [(0, 1), (1, 0)])


def turned(value, steps):
    count = lax.axis_size("mp")
    return lax.ppermute(value, "mp", [(i, (i + steps) % count) for i in range(count)])


def exchanged(value):
    return lax.all_to_all(value, "dp", split_axis=0, concat_axis=0, tiled=True)


def along_x(value, steps):
    pairs = [
        (x * Z_CHIPS + z, (x + steps) % X_CHIPS * Z_CHIPS + z)
        for x in range(X_CHIPS)
        for z in range(Z_CHIPS)
    ]
    return lax.ppermute(value, "dp", pairs)


def along_z(value, steps):
    pairs = [
        (x * Z_CHIPS + z, x * Z_CHIPS + (z + steps) % Z_CHIPS)
        for x in range(X_CHIPS)
        for z in range(Z_CHIPS)
    ]
    return lax.ppermute(value, "dp", pairs)


def gathered_in(value, across):
    columns = [[x * Z_CHIPS + z for z in range(Z_CHIPS)] for x in range(X_CHIPS)]
    rows = [[x * Z_CHIPS + z for x in range(X_CHIPS)] for z in range(Z_CHIPS)]
    groups = rows if across else columns
    return lax.all_gather(value, "dp", axis=0, tiled=True, axis_index_groups=groups)


KEY_VALUE = ((True, (0, 1)), (False, (0, 1)))
QUERY_OUT = ((False, (0,)), (True, (1,)))
QUERY = ((False, (0,)), (True, (0,)))


def per_device(tokens, passages, weights, cotangent, neighbours, passage_home, request_lists):
    own_index = lax.axis_index("dp")
    section = lax.axis_index("section")
    group = lax.axis_index("mp")
    groups = lax.axis_size("mp")
    peers = lax.axis_size("dp")
    leading = section == 0
    per_owner, length, width = passages.shape
    half = weights.shape[3] // 2
    row_count = tokens.shape[0]
    block_count = neighbours.shape[0]
    here = jnp.stack([section, group, own_index]).astype(jnp.int32)

    start = jnp.where(leading, tokens, cotangent)
    near_start, far_start = (start[: row_count // 2], start[row_count // 2 :])
    near_parts = [near_start] + [turned(near_start, k) for k in range(1, groups)]
    tables = integers(
        lambda *refs: lists_kernel(per_owner, *refs),
        (1, peers, peers, 2 * peers, peers, peers, request_lists.shape[1]),
        here,
        passage_home,
        request_lists,
    )
    far_start, near_parts, tables = lax.optimization_barrier((far_start, near_parts, tables))
    count, lists, local, spots, unit_of, place_of, owners = tables
    far_parts = [far_start] + [turned(far_start, k) for k in range(1, groups)]
    own = weights[0]
    other = swapped(own)

    def own_rows(kept, got):
        return jnp.concatenate(
            [jnp.where(leading, kept, got), jnp.where(leading, got, kept)], axis=1
        )

    def moved(pair):
        return (along_z(pair[0], 1), along_z(pair[1], -1))

    pointers = neighbours.reshape(-1)
    shown = jnp.pad(
        pointers.astype(jnp.bfloat16)[None, :], ((0, 15), (0, 2 * half - pointers.shape[0]))
    )
    kept, sent = project(QUERY_OUT, here, own, other, near_parts)
    near = jnp.concatenate([own_rows(kept, swapped(sent)), shown], axis=0)
    lines = [None] * Z_CHIPS
    lines[0] = near
    step = moved((near, near))
    step, far_parts[1] = lax.optimization_barrier((step, far_parts[1]))
    lines[Z_CHIPS - 1], lines[1] = step
    step = moved(step)
    step, far_parts[2], far_parts[3] = lax.optimization_barrier((step, far_parts[2], far_parts[3]))
    lines[Z_CHIPS - 2], lines[2] = step
    step = moved(step)
    kept, sent = project(QUERY_OUT, here, own, other, far_parts)
    step, kept, sent = lax.optimization_barrier((step, kept, sent))
    lines[Z_CHIPS - 3], lines[3] = step
    cut = near.shape[0] - BLOCK
    last = (along_z(step[0][:cut], 1), along_z(step[1][cut:], -1))
    last, kept, got = lax.optimization_barrier((last, kept, swapped(sent)))
    lines[Z_CHIPS // 2] = jnp.concatenate(last, axis=0)
    far = own_rows(kept, got)
    near = gathered_in(jnp.concatenate(lines, axis=0), True)
    near = near.reshape(peers, row_count // 2 + 16, 2 * half)
    shown = near[:, row_count // 2, : pointers.shape[0]].astype(jnp.int32)

    flat = passages.reshape(per_owner * length, width)
    half_rows = per_owner * length // 2
    held = lax.dynamic_slice_in_dim(flat, section * half_rows, half_rows, 0)
    held, far = lax.optimization_barrier((held, far))
    unit = jnp.stack([far] + [along_x(far, k) for k in range(1, X_CHIPS)])
    units = [None] * (Z_CHIPS + 1)
    units[0] = unit
    ahead, behind = (along_z(unit, 1), along_z(unit, -1))
    held_parts = [held] + [turned(held, k) for k in range(1, groups)]
    ahead, behind, held_parts[1], held_parts[3] = lax.optimization_barrier(
        (ahead, behind, held_parts[1], held_parts[3])
    )
    units[Z_CHIPS - 1], units[1] = (ahead, behind)
    ahead, behind = (along_z(ahead, 1), along_z(behind, -1))
    ahead, behind, held_parts[2] = lax.optimization_barrier((ahead, behind, held_parts[2]))
    units[Z_CHIPS - 2], units[2] = (ahead, behind)
    ahead, behind = (along_z(ahead, 1), along_z(behind, -1))
    kept, sent = project(KEY_VALUE, here, own, other, held_parts)
    ahead, behind, kept, sent = lax.optimization_barrier((ahead, behind, kept, sent))
    units[Z_CHIPS - 3], units[3] = (ahead, behind)
    middle = X_CHIPS // 2
    units[Z_CHIPS // 2] = along_z(ahead[:middle], 1)
    units[Z_CHIPS] = along_z(behind[middle:], -1)
    got = swapped(sent)
    kv = jnp.concatenate(
        [jnp.where(leading, kept, got), jnp.where(leading, got, kept)], axis=0
    ).reshape(per_owner, length, 2 * half)

    blocks, line, owner_of, slot_of = integers(
        blocks_kernel,
        (2 * peers, peers, pointers.shape[0], pointers.shape[0]),
        here,
        count,
        spots,
        owners,
        shown,
    )
    routes = (count, lists, local)
    sources = (blocks, line, unit_of, place_of)
    places = owner_of * 2 + slot_of
    asked, stats = list_stats(routes, sources, near, units, kv)
    joint = exchanged(combine(owner_of, slot_of, exchanged(stats)))
    query_slots = list_queries(routes, asked, kv, joint)
    returned = exchanged(query_slots).reshape(2 * peers, BLOCK, half)
    stored = list_stored(routes, asked, kv, joint)

    def summed(terms):
        total = terms[0].astype(jnp.float32)
        for k in range(1, groups):
            total = total + turned(terms[k], k).astype(jnp.float32)
        return total.astype(jnp.bfloat16)

    stored = stored.reshape(per_owner * length, 2 * half)
    passage_terms = features(KEY_VALUE, here, own, other, stored, swapped(stored))
    passage_grad = summed(passage_terms).reshape(per_owner, length, width // 2)

    terms = jnp.take(returned, places, axis=0, mode="clip").reshape(block_count, 2, BLOCK, half)
    query_grad = (terms[:, 0].astype(jnp.float32) + terms[:, 1].astype(jnp.float32)).astype(
        jnp.bfloat16
    )
    query_grad = query_grad.reshape(row_count, half)
    token_terms = features(QUERY, here, own, other, query_grad, swapped(query_grad))
    return (summed(token_terms), passage_grad)


def solution(mesh):
    in_specs = (
        P("dp", "mp"),
        P("dp", None, "mp"),
        P("section", None, None, "mp"),
        P("dp", "mp"),
        P("dp", None),
        P(),
        P(),
    )
    out_specs = (P("dp", ("section", "mp")), P("dp", None, ("section", "mp")))
    return jax.shard_map(
        per_device, mesh=mesh, in_specs=in_specs, out_specs=out_specs, check_vma=False
    )
```

```python
import math

import jax
import jax.numpy as jnp
from jax import lax
from jax.experimental import pallas as pl
from jax.experimental.pallas import tpu as pltpu
from jax.sharding import PartitionSpec as P

HEAD_DIM = 128
BLOCK = 64
X_CHIPS = 4
Z_CHIPS = 8
SCALE = 1.0 / math.sqrt(HEAD_DIM)
UNUSED = 1e30
VMEM = pl.BlockSpec(memory_space=pltpu.VMEM)
SMEM = pl.BlockSpec(memory_space=pltpu.SMEM)
ANY = pl.BlockSpec(memory_space=pl.ANY)
PARAMS = pltpu.CompilerParams(vmem_limit_bytes=56 * 1024 * 1024)


def cost(flops, moved):
    return pl.CostEstimate(flops=int(flops), bytes_accessed=int(moved), transcendentals=0)


def rows_by_rows(left, right):
    return lax.dot_general(left, right, (((1,), (1,)), ((), ())), preferred_element_type=jnp.float32)


def lists_kernel(
    per_owner, here, home, wanted, count, lists, local, spots, unit, place, owners
):
    peers, listed = wanted.shape
    own = here[2]
    lowest = own * per_owner
    own_x, own_z = (lax.div(own, Z_CHIPS), lax.rem(own, Z_CHIPS))

    def one_list(j, found):
        position, held_at = (-1, 0)
        for u in range(listed):
            row = home[wanted[j, u]] - lowest
            hit = (row >= 0) & (row < per_owner)
            position = jnp.where(hit, u, position)
            held_at = jnp.where(hit, row, held_at)
        behind_z = lax.rem(lax.rem(j, Z_CHIPS) - own_z + Z_CHIPS, Z_CHIPS)
        behind_x = lax.rem(own_x - lax.div(j, Z_CHIPS) + X_CHIPS, X_CHIPS)

        @pl.when(position >= 0)
        def _():
            lists[found] = j
            local[found] = held_at
            spots[2 * found] = position
            spots[2 * found + 1] = lax.div(j, Z_CHIPS) * Z_CHIPS + behind_z
            split = (behind_z == Z_CHIPS // 2) & (behind_x >= X_CHIPS // 2)
            unit[found] = jnp.where(split, Z_CHIPS, behind_z)
            place[found] = jnp.where(split, behind_x - X_CHIPS // 2, behind_x)

        return found + jnp.where(position >= 0, 1, 0)

    count[0] = lax.fori_loop(0, peers, one_list, 0)
    for u in range(listed):
        owners[u] = lax.div(home[wanted[own, u]], per_owner)


def blocks_kernel(here, count, spots, owners, shown, blocks, line, owner_of, slot_of):
    refs = shown.shape[1]
    own_row = lax.div(here[2], Z_CHIPS) * Z_CHIPS

    def one_list(i, carry):
        position, row = (spots[2 * i], spots[2 * i + 1])
        first, last = (refs - 1, 0)
        for ref in range(refs):
            last = jnp.where(shown[row, ref] == position, ref, last)
            back = refs - 1 - ref
            first = jnp.where(shown[row, back] == position, back, first)
        blocks[2 * i] = lax.div(first, 2)
        blocks[2 * i + 1] = lax.div(last, 2)
        line[i] = row
        return carry

    lax.fori_loop(0, count[0], one_list, 0)
    for ref in range(refs):
        pointer = shown[own_row, ref]
        owner_of[ref] = owners[pointer]
        slot = 0
        for before in range(ref):
            slot = jnp.where(shown[own_row, before] == pointer, 1, slot)
        slot_of[ref] = slot


def integers(kernel, sizes, *args):
    return pl.pallas_call(
        kernel,
        out_shape=tuple(jax.ShapeDtypeStruct((size,), jnp.int32) for size in sizes),
        in_specs=[SMEM] * len(args),
        out_specs=(SMEM,) * len(sizes),
        compiler_params=PARAMS,
    )(*args)


def start_by_section(section, choices, copy_from):
    for which, weights_ref in enumerate(choices):

        @pl.when(section == which)
        def _():
            copy_from(which, weights_ref).start()


def project_kernel(picks, here, own_ref, other_ref, *refs):
    parts = refs[:4]
    keep_ref, send_ref, held, sems = refs[-4:]
    section, group = (here[0], here[1])
    depth = parts[0].shape[1]
    mats = len(picks[0][1])
    half = held.shape[3] // 2

    def fetch(which, source, mat, k):
        low = pl.multiple_of((group - k + 4) % 4 * depth, depth)
        return pltpu.make_async_copy(
            source.at[picks[which][1][mat], pl.ds(low, depth), :],
            held.at[mat, k],
            sems.at[mat * 4 + k],
        )

    for k in range(4):
        for mat in range(mats):
            start_by_section(
                section,
                [own_ref if picks[which][0] else other_ref for which in range(2)],
                lambda which, source: fetch(which, source, mat, k),
            )
    for mat in range(mats):
        total = None
        for k in range(4):
            fetch(0, own_ref, mat, k).wait()
            term = jnp.dot(parts[k][...], held[mat, k], preferred_element_type=jnp.float32)
            total = term if total is None else total + term
        low, high = (total[:, :half].astype(jnp.bfloat16), total[:, half:].astype(jnp.bfloat16))
        columns = pl.ds(mat * half, half)

        @pl.when(section == 0)
        def _():
            keep_ref[:, columns] = low
            send_ref[:, columns] = high

        @pl.when(section == 1)
        def _():
            keep_ref[:, columns] = high
            send_ref[:, columns] = low


def project(picks, here, own, other, parts, after=()):
    rows, depth = parts[0].shape
    mats = len(picks[0][1])
    cols = own.shape[2]
    out = jax.ShapeDtypeStruct((rows, mats * cols // 2), jnp.bfloat16)
    return pl.pallas_call(
        lambda *refs: project_kernel(picks, *refs),
        out_shape=(out, out),
        in_specs=[SMEM, ANY, ANY] + [VMEM] * 4 + [ANY] * len(after),
        out_specs=(VMEM, VMEM),
        scratch_shapes=[
            pltpu.VMEM((mats, 4, depth, cols), jnp.bfloat16),
            pltpu.SemaphoreType.DMA((mats * 4,)),
        ],
        compiler_params=PARAMS,
        cost_estimate=cost(8 * rows * depth * cols * mats, 8 * depth * cols * mats),
    )(here, own, other, *parts, *after)


def features_kernel(picks, here, own_ref, other_ref, mine_ref, got_ref, *refs):
    outs = refs[:4]
    held, sems = refs[4:]
    section, group = (here[0], here[1])
    mats, _, _, chunk, half = held.shape

    def fetch(which, source, mat, side, k):
        low = pl.multiple_of((section * 4 + (group + k) % 4) * chunk, chunk)
        left = which * half if side == 0 else (1 - which) * half
        return pltpu.make_async_copy(
            source.at[picks[which][1][mat], pl.ds(low, chunk), pl.ds(left, half)],
            held.at[mat, side, k],
            sems.at[(mat * 2 + side) * 4 + k],
        )

    order = (2, 1, 3, 0)
    for k in order:
        for mat in range(mats):
            for side in range(2):
                start_by_section(
                    section,
                    [own_ref if picks[which][0] else other_ref for which in range(2)],
                    lambda which, source: fetch(which, source, mat, side, k),
                )
    for k in order:
        total = None
        for mat in range(mats):
            for side, grads in enumerate((mine_ref, got_ref)):
                fetch(0, own_ref, mat, side, k).wait()
                term = rows_by_rows(grads[:, mat * half : (mat + 1) * half], held[mat, side, k])
                total = term if total is None else total + term
        outs[k][...] = total.astype(jnp.bfloat16)


def features(picks, here, own, other, mine, got):
    rows = mine.shape[0]
    mats = len(picks[0][1])
    half = mine.shape[1] // mats
    chunk = own.shape[1] // 8
    out = jax.ShapeDtypeStruct((rows, chunk), jnp.bfloat16)
    return pl.pallas_call(
        lambda *refs: features_kernel(picks, *refs),
        out_shape=(out,) * 4,
        in_specs=[SMEM, ANY, ANY, VMEM, VMEM],
        out_specs=(VMEM,) * 4,
        scratch_shapes=[
            pltpu.VMEM((mats, 2, 4, chunk, half), jnp.bfloat16),
            pltpu.SemaphoreType.DMA((mats * 8,)),
        ],
        compiler_params=PARAMS,
        cost_estimate=cost(16 * rows * chunk * half * mats, 16 * chunk * half * mats),
    )(here, own, other, mine, got)


def head_views(rows_ref, kv_ref, i, passage, head, heads):
    width = heads * HEAD_DIM
    first = pl.ds(head * HEAD_DIM, HEAD_DIM)
    second = pl.ds(width + head * HEAD_DIM, HEAD_DIM)
    return (
        rows_ref[i, :, first],
        rows_ref[i, :, second],
        kv_ref[passage, :, first],
        kv_ref[passage, :, second],
    )


def chains(first, second, heads):
    return [(item, head) for item in (first, second) for head in range(heads)]


def over_pairs(count, body):
    def step(t, carry):
        return body(2 * t, jnp.minimum(2 * t + 1, count - 1), carry)

    lax.fori_loop(0, lax.div(count + 1, 2), step, 0)


def start_all(count, copy_of):
    def step(i, carry):
        copy_of(i).start()
        return carry

    lax.fori_loop(0, count, step, 0)


def wait_all(count, copy_of):
    def step(i, carry):
        copy_of(i).wait()
        return carry

    lax.fori_loop(0, count, step, 0)


def wait_pair(i, second, copy_of):
    copy_of(i).wait()

    @pl.when(second > i)
    def _():
        copy_of(second).wait()


def stats_kernel(count, lists, local, blocks, line, unit, place, near_ref, *refs):
    far_refs = refs[: Z_CHIPS + 1]
    kv_ref, rows_out, out_ref, rows_ref, sems, out_sems = refs[Z_CHIPS + 1 :]
    heads = rows_ref.shape[2] // (2 * HEAD_DIM)
    held = near_ref.shape[1] // BLOCK
    out_ref[...] = jnp.zeros_like(out_ref)

    def fetch(source, first, row, i, slot):
        low = pl.multiple_of(row * BLOCK, BLOCK)
        return pltpu.make_async_copy(
            source.at[first, pl.ds(low, BLOCK), :],
            rows_ref.at[i, pl.ds(slot * BLOCK, BLOCK), :],
            sems.at[2 * i + slot],
        )

    def ask(i, carry):
        for slot in range(2):
            block = blocks[2 * i + slot]

            @pl.when(block < held)
            def _():
                fetch(near_ref, line[i], block, i, slot).start()

            for which, far_ref in enumerate(far_refs):

                @pl.when((block >= held) & (unit[i] == which))
                def _():
                    fetch(far_ref, place[i], block - held, i, slot).start()

        return carry

    lax.fori_loop(0, count[0], ask, 0)

    def keep(i):
        return pltpu.make_async_copy(rows_ref.at[i], rows_out.at[i], out_sems.at[i])

    def arrive(i):
        for slot in range(2):
            fetch(near_ref, 0, 0, i, slot).wait()
        keep(i).start()

    def one_pair(i, second, carry):
        arrive(i)

        @pl.when(second > i)
        def _():
            arrive(second)

        items = chains(i, second, heads)
        parts = [head_views(rows_ref, kv_ref, item, local[item], head, heads) for item, head in items]
        scores = [rows_by_rows(key, query) * SCALE for query, _, key, _ in parts]
        prob_grads = [rows_by_rows(value, grad) for _, grad, _, value in parts]
        tops = [jnp.max(score, axis=0, keepdims=True) for score in scores]
        raised = [jnp.exp(score - top) for score, top in zip(scores, tops)]
        totals = [jnp.sum(part, axis=0, keepdims=True) for part in raised]
        inners = [
            jnp.sum(part * prob_grad, axis=0, keepdims=True) / total
            for part, prob_grad, total in zip(raised, prob_grads, totals)
        ]
        found = [
            (item, head, top + jnp.log(total), inner)
            for (item, head), top, total, inner in zip(items, tops, totals, inners)
        ]
        for item, head, logs, inner in found:
            out_ref[lists[item], 2 * head : 2 * head + 1, :] = logs
            out_ref[lists[item], 2 * head + 1 : 2 * head + 2, :] = inner
        return carry

    over_pairs(count[0], one_pair)
    wait_all(count[0], keep)


def list_stats(routes, sources, near, far, kv):
    lists = routes[1].shape[0]
    return pl.pallas_call(
        stats_kernel,
        out_shape=(
            jax.ShapeDtypeStruct((lists, 2 * BLOCK, near.shape[2]), jnp.bfloat16),
            jax.ShapeDtypeStruct((lists, 8, 2 * BLOCK), jnp.float32),
        ),
        in_specs=[SMEM] * 7 + [ANY] * (Z_CHIPS + 2) + [VMEM],
        out_specs=(ANY, VMEM),
        scratch_shapes=[
            pltpu.VMEM((lists, 2 * BLOCK, near.shape[2]), jnp.bfloat16),
            pltpu.SemaphoreType.DMA((2 * lists,)),
            pltpu.SemaphoreType.DMA((lists,)),
        ],
        compiler_params=PARAMS,
    )(*routes, *sources, near, *far, kv)


def combine_kernel(owner_of, slot_of, stats_ref, out_ref):
    sub = lax.broadcasted_iota(jnp.int32, stats_ref.shape[1:], 0)
    lane = lax.broadcasted_iota(jnp.int32, stats_ref.shape[1:], 1)
    even = sub % 2 == 0
    out_ref[...] = jnp.broadcast_to(jnp.where(even, UNUSED, 0.0)[None], out_ref.shape)
    for block in range(owner_of.shape[0] // 2):
        refs = (2 * block, 2 * block + 1)
        logs, inners = ([], [])
        for ref in refs:
            row = stats_ref[owner_of[ref]]
            row = jnp.where(slot_of[ref] == 0, row, pltpu.roll(row, BLOCK, 1))
            logs.append(row)
            inners.append(pltpu.roll(row, 7, 0))
        top = jnp.maximum(logs[0], logs[1])
        first, second = (jnp.exp(logs[0] - top), jnp.exp(logs[1] - top))
        total = first + second
        joint = (first * inners[0] + second * inners[1]) / total
        both = jnp.where(even, top + jnp.log(total), pltpu.roll(joint, 1, 0))
        both = jnp.where(lane < BLOCK, both, pltpu.roll(both, BLOCK, 1))
        for ref in refs:
            place = owner_of[ref]
            half = jnp.where(lane < BLOCK, 0, 1)
            out_ref[place] = jnp.where(half == slot_of[ref], both, out_ref[place])


def combine(owner_of, slot_of, stats):
    return pl.pallas_call(
        combine_kernel,
        out_shape=jax.ShapeDtypeStruct(stats.shape, jnp.float32),
        in_specs=[SMEM, SMEM, VMEM],
        out_specs=VMEM,
        compiler_params=PARAMS,
    )(owner_of, slot_of, stats)


def score_terms(rows_ref, kv_ref, joint_ref, lists, local, items, heads):
    parts = [head_views(rows_ref, kv_ref, i, local[i], head, heads) for i, head in items]
    scores = [rows_by_rows(key, query) for query, _, key, _ in parts]
    prob_grads = [rows_by_rows(value, grad) for _, grad, _, value in parts]
    logs = [joint_ref[lists[i], 2 * head : 2 * head + 1, :] for i, head in items]
    inners = [joint_ref[lists[i], 2 * head + 1 : 2 * head + 2, :] for i, head in items]
    probs = [jnp.exp(score * SCALE - log) for score, log in zip(scores, logs)]
    score_grads = [
        (prob * (prob_grad - inner) * SCALE).astype(jnp.bfloat16)
        for prob, prob_grad, inner in zip(probs, prob_grads, inners)
    ]
    return (parts, probs, score_grads)


def query_kernel(
    count, lists, local, rows_in, kv_ref, joint_ref, query_out, rows_ref, held, sems, out_sems
):
    heads = rows_ref.shape[2] // (2 * HEAD_DIM)

    def fetch(i):
        return pltpu.make_async_copy(rows_in.at[i], rows_ref.at[i], sems.at[i])

    def give(i):
        return pltpu.make_async_copy(held.at[i], query_out.at[lists[i]], out_sems.at[i])

    start_all(count[0], fetch)

    def one_pair(i, second, carry):
        wait_pair(i, second, fetch)
        items = chains(i, second, heads)
        parts, _, score_grads = score_terms(
            rows_ref, kv_ref, joint_ref, lists, local, items, heads
        )
        query_grads = [
            lax.dot_general(
                score_grad, part[2], (((0,), (0,)), ((), ())), preferred_element_type=jnp.float32
            )
            for score_grad, part in zip(score_grads, parts)
        ]
        for (item, head), query_grad in zip(items, query_grads):
            held[item, :, pl.ds(head * HEAD_DIM, HEAD_DIM)] = query_grad.astype(jnp.bfloat16)
        give(i).start()

        @pl.when(second > i)
        def _():
            give(second).start()

        return carry

    over_pairs(count[0], one_pair)
    wait_all(count[0], give)


def list_queries(routes, rows, kv, joint):
    lists, depth, width = rows.shape
    return pl.pallas_call(
        query_kernel,
        out_shape=jax.ShapeDtypeStruct((lists, depth, width // 2), jnp.bfloat16),
        in_specs=[SMEM] * 3 + [ANY, VMEM, VMEM],
        out_specs=ANY,
        scratch_shapes=[
            pltpu.VMEM(rows.shape, jnp.bfloat16),
            pltpu.VMEM((lists, depth, width // 2), jnp.bfloat16),
            pltpu.SemaphoreType.DMA((lists,)),
            pltpu.SemaphoreType.DMA((lists,)),
        ],
        compiler_params=PARAMS,
    )(*routes, rows, kv, joint)


def stored_kernel(
    count, lists, local, rows_in, kv_ref, joint_ref, stored_out, total, rows_ref, sems
):
    heads = rows_ref.shape[2] // (2 * HEAD_DIM)
    width = heads * HEAD_DIM

    def fetch(i):
        return pltpu.make_async_copy(rows_in.at[i], rows_ref.at[i], sems.at[i])

    start_all(count[0], fetch)
    total[...] = jnp.zeros_like(total)

    def add_rounded(passage, low, term):
        place = (passage, slice(None), pl.ds(low, HEAD_DIM))
        total[place] += term.astype(jnp.bfloat16).astype(jnp.float32)

    def one_pair(i, second, carry):
        wait_pair(i, second, fetch)
        items = chains(i, second, heads)
        parts, probs, score_grads = score_terms(
            rows_ref, kv_ref, joint_ref, lists, local, items, heads
        )
        found = [
            (
                head * HEAD_DIM,
                jnp.dot(score_grad, part[0], preferred_element_type=jnp.float32),
                jnp.dot(prob.astype(jnp.bfloat16), part[1], preferred_element_type=jnp.float32),
            )
            for (_, head), part, prob, score_grad in zip(items, parts, probs, score_grads)
        ]
        for low, key_term, value_term in found[:heads]:
            add_rounded(local[i], low, key_term)
            add_rounded(local[i], width + low, value_term)

        @pl.when(second > i)
        def _():
            for low, key_term, value_term in found[heads:]:
                add_rounded(local[second], low, key_term)
                add_rounded(local[second], width + low, value_term)

        return carry

    over_pairs(count[0], one_pair)
    stored_out[...] = total[...].astype(jnp.bfloat16)


def list_stored(routes, rows, kv, joint):
    return pl.pallas_call(
        stored_kernel,
        out_shape=jax.ShapeDtypeStruct(kv.shape, jnp.bfloat16),
        in_specs=[SMEM] * 3 + [ANY, VMEM, VMEM],
        out_specs=VMEM,
        scratch_shapes=[
            pltpu.VMEM(kv.shape, jnp.float32),
            pltpu.VMEM(rows.shape, jnp.bfloat16),
            pltpu.SemaphoreType.DMA((rows.shape[0],)),
        ],
        compiler_params=PARAMS,
        cost_estimate=cost(8 * rows.size * HEAD_DIM, 4 * rows.size),
    )(*routes, rows, kv, joint)


def swapped(value):
    return lax.ppermute(value, "section", [(0, 1), (1, 0)])


def turned(value, steps):
    count = lax.axis_size("mp")
    return lax.ppermute(value, "mp", [(i, (i + steps) % count) for i in range(count)])


def exchanged(value):
    return lax.all_to_all(value, "dp", split_axis=0, concat_axis=0, tiled=True)


def along_x(value, steps):
    pairs = [
        (x * Z_CHIPS + z, (x + steps) % X_CHIPS * Z_CHIPS + z)
        for x in range(X_CHIPS)
        for z in range(Z_CHIPS)
    ]
    return lax.ppermute(value, "dp", pairs)


def along_z(value, steps):
    pairs = [
        (x * Z_CHIPS + z, x * Z_CHIPS + (z + steps) % Z_CHIPS)
        for x in range(X_CHIPS)
        for z in range(Z_CHIPS)
    ]
    return lax.ppermute(value, "dp", pairs)


def gathered_in(value, across):
    columns = [[x * Z_CHIPS + z for z in range(Z_CHIPS)] for x in range(X_CHIPS)]
    rows = [[x * Z_CHIPS + z for x in range(X_CHIPS)] for z in range(Z_CHIPS)]
    groups = rows if across else columns
    return lax.all_gather(value, "dp", axis=0, tiled=True, axis_index_groups=groups)


KEY_VALUE = ((True, (0, 1)), (False, (0, 1)))
QUERY_OUT = ((False, (0,)), (True, (1,)))
QUERY = ((False, (0,)), (True, (0,)))


def per_device(tokens, passages, weights, cotangent, neighbours, passage_home, request_lists):
    own_index = lax.axis_index("dp")
    section = lax.axis_index("section")
    group = lax.axis_index("mp")
    groups = lax.axis_size("mp")
    peers = lax.axis_size("dp")
    leading = section == 0
    per_owner, length, width = passages.shape
    half = weights.shape[3] // 2
    row_count = tokens.shape[0]
    block_count = neighbours.shape[0]
    here = jnp.stack([section, group, own_index]).astype(jnp.int32)

    near_start, far_start = (
        jnp.where(leading, tokens[rows], cotangent[rows])
        for rows in (slice(0, row_count // 2), slice(row_count // 2, row_count))
    )
    near_parts = [near_start] + [turned(near_start, k) for k in range(1, groups)]
    tables = integers(
        lambda *refs: lists_kernel(per_owner, *refs),
        (1, peers, peers, 2 * peers, peers, peers, request_lists.shape[1]),
        here,
        passage_home,
        request_lists,
    )
    far_start, near_parts, tables = lax.optimization_barrier((far_start, near_parts, tables))
    count, lists, local, spots, unit_of, place_of, owners = tables
    far_parts = [far_start] + [turned(far_start, k) for k in range(1, groups)]
    own = weights[0]
    other = swapped(own)

    def own_rows(kept, got):
        return jnp.concatenate(
            [jnp.where(leading, kept, got), jnp.where(leading, got, kept)], axis=1
        )

    def moved(pair):
        return (along_z(pair[0], 1), along_z(pair[1], -1))

    pointers = neighbours.reshape(-1)
    shown = jnp.pad(
        pointers.astype(jnp.bfloat16)[None, :], ((0, 15), (0, 2 * half - pointers.shape[0]))
    )
    kept, sent = project(QUERY_OUT, here, own, other, near_parts)
    near = jnp.concatenate([own_rows(kept, swapped(sent)), shown], axis=0)
    lines = [None] * Z_CHIPS
    lines[0] = near
    step = moved((near, near))
    step, far_parts[1] = lax.optimization_barrier((step, far_parts[1]))
    lines[Z_CHIPS - 1], lines[1] = step
    step = moved(step)
    step, far_parts[2], far_parts[3] = lax.optimization_barrier((step, far_parts[2], far_parts[3]))
    lines[Z_CHIPS - 2], lines[2] = step
    step = moved(step)
    kept, sent = project(QUERY_OUT, here, own, other, far_parts)
    step, kept, sent = lax.optimization_barrier((step, kept, sent))
    lines[Z_CHIPS - 3], lines[3] = step
    cut = near.shape[0] - BLOCK
    last = (along_z(step[0][:cut], 1), along_z(step[1][cut:], -1))
    last, kept, got = lax.optimization_barrier((last, kept, swapped(sent)))
    lines[Z_CHIPS // 2] = jnp.concatenate(last, axis=0)
    far = own_rows(kept, got)
    near = gathered_in(jnp.concatenate(lines, axis=0), True)
    near = near.reshape(peers, row_count // 2 + 16, 2 * half)
    shown = near[:, row_count // 2, : pointers.shape[0]].astype(jnp.int32)

    flat = passages.reshape(per_owner * length, width)
    half_rows = per_owner * length // 2
    held = lax.dynamic_slice_in_dim(flat, section * half_rows, half_rows, 0)
    held, far = lax.optimization_barrier((held, far))
    unit = jnp.stack([far] + [along_x(far, k) for k in range(1, X_CHIPS)])
    units = [None] * (Z_CHIPS + 1)
    units[0] = unit
    ahead, behind = (along_z(unit, 1), along_z(unit, -1))
    held_parts = [held] + [turned(held, k) for k in range(1, groups)]
    ahead, behind, held_parts[1], held_parts[3] = lax.optimization_barrier(
        (ahead, behind, held_parts[1], held_parts[3])
    )
    units[Z_CHIPS - 1], units[1] = (ahead, behind)
    ahead, behind = (along_z(ahead, 1), along_z(behind, -1))
    ahead, behind, held_parts[2] = lax.optimization_barrier((ahead, behind, held_parts[2]))
    units[Z_CHIPS - 2], units[2] = (ahead, behind)
    ahead, behind = (along_z(ahead, 1), along_z(behind, -1))
    kept, sent = project(KEY_VALUE, here, own, other, held_parts)
    ahead, behind, kept, sent = lax.optimization_barrier((ahead, behind, kept, sent))
    units[Z_CHIPS - 3], units[3] = (ahead, behind)
    middle = X_CHIPS // 2
    units[Z_CHIPS // 2] = along_z(ahead[:middle], 1)
    units[Z_CHIPS] = along_z(behind[middle:], -1)
    got = swapped(sent)
    kv = jnp.concatenate(
        [jnp.where(leading, kept, got), jnp.where(leading, got, kept)], axis=0
    ).reshape(per_owner, length, 2 * half)

    blocks, line, owner_of, slot_of = integers(
        blocks_kernel,
        (2 * peers, peers, pointers.shape[0], pointers.shape[0]),
        here,
        count,
        spots,
        owners,
        shown,
    )
    routes = (count, lists, local)
    sources = (blocks, line, unit_of, place_of)
    places = owner_of * 2 + slot_of
    asked, stats = list_stats(routes, sources, near, units, kv)
    joint = exchanged(combine(owner_of, slot_of, exchanged(stats)))
    query_slots = list_queries(routes, asked, kv, joint)
    returned = exchanged(query_slots).reshape(2 * peers, BLOCK, half)
    stored = list_stored(routes, asked, kv, joint)

    def summed(terms):
        total = terms[0].astype(jnp.float32)
        for k in range(1, groups):
            total = total + turned(terms[k], k).astype(jnp.float32)
        return total.astype(jnp.bfloat16)

    stored = stored.reshape(per_owner * length, 2 * half)
    passage_terms = features(KEY_VALUE, here, own, other, stored, swapped(stored))
    passage_grad = summed(passage_terms).reshape(per_owner, length, width // 2)

    terms = jnp.take(returned, places, axis=0, mode="clip").reshape(block_count, 2, BLOCK, half)
    query_grad = (terms[:, 0].astype(jnp.float32) + terms[:, 1].astype(jnp.float32)).astype(
        jnp.bfloat16
    )
    query_grad = query_grad.reshape(row_count, half)
    token_terms = features(QUERY, here, own, other, query_grad, swapped(query_grad))
    return (summed(token_terms), passage_grad)


def solution(mesh):
    in_specs = (
        P("dp", "mp"),
        P("dp", None, "mp"),
        P("section", None, None, "mp"),
        P("dp", "mp"),
        P("dp", None),
        P(),
        P(),
    )
    out_specs = (P("dp", ("section", "mp")), P("dp", None, ("section", "mp")))
    return jax.shard_map(
        per_device, mesh=mesh, in_specs=in_specs, out_specs=out_specs, check_vma=False
    )
```
